512 devices in a mesh: round: 8 (over x, core), brick: 64 (over y, z).
Axes of the slice: x: 4, y: 4, z: 16, core: 2. Of those that a mesh axis runs over, the one named last changes fastest.
Arguments:
- image: bfloat16 [8, 512, 4, 32, 8, 128], P('round', 'brick'), may hold values from -60 to 60
- shifts: int32 [8, 512], P('round', 'brick'), may hold values from -24 to 24, as said below
- fractions: float32 [8, 512], P('round', 'brick'), may hold values from 0 to 1
- valid: int32 [512], replicated, may hold values from 0 to 1, as said below
Outputs:
- spots: bfloat16 [8, 8, 64, 4, 32, 8, 128], P(None, 'round', 'brick')
The draws below stay inside these ranges and needn't reach their ends.
Inputs may be any that keep to these rules, and one draw needn't show every extreme that they name: `shifts`: in every round, the last brick of each aligned block of 8 bricks has a shift between minus 24 and minus half of 24 (rounded down), and the first brick of each such block a shift between half of 24 (rounded down) and 24. `valid`: the first and the last brick of each aligned block of 8 bricks hold tissue.
All inputs are finite; a program needn't handle non-finite values.
Results may differ from the reference program's by a relative error of at most 0.0055.
Values may be sent and summed in bfloat16 or wider, within the bound.
A program may use at most 128 MiB of HBM per device.

```python
import jax
import jax.numpy as jnp
from jax import lax

CHANNELS = 4
DEPTH = 32
HEIGHT = 8
WIDTH = 128
SMAX = 24
BRK_DEV = 8
ROUNDS = 8
BRICKS = 512
N_ROUND = 8
N_BRICK = 64


def draw_image(key, part):
    first, second = jax.random.split(jax.random.fold_in(key, 11))
    shape = (ROUNDS, BRICKS, CHANNELS, DEPTH, HEIGHT, WIDTH)
    rise = 1.0 + 2.0 * jnp.arange(BRICKS, dtype=jnp.float32) / max(BRICKS - 1, 1)
    noise = jnp.clip(jax.random.normal(first, shape, jnp.float32), -6.0, 6.0)
    plane = jnp.exp(jax.random.uniform(second, (ROUNDS, BRICKS, CHANNELS, 1, HEIGHT, 1), jnp.float32, 0.0, 1.098612))
    values = noise * plane * rise[None, :, None, None, None, None]
    return values.astype(jnp.bfloat16)


def draw_shifts(key, part):
    common = jax.random.randint(jax.random.fold_in(key, 21), (ROUNDS, BRICKS), 0 - SMAX, SMAX + 1)
    strong = jax.random.randint(jax.random.fold_in(key, 22), (ROUNDS, BRICKS), SMAX // 2, SMAX + 1)
    position = jnp.arange(BRICKS, dtype=jnp.int32) % BRK_DEV
    result = jnp.where(position[None, :] == BRK_DEV - 1, 0 - strong, common)
    result = jnp.where(position[None, :] == 0, strong, result)
    return result.astype(jnp.int32)


def draw_valid(key, part):
    pick = jax.random.randint(jax.random.fold_in(key, 31), (BRICKS,), 0, 4)
    position = jnp.arange(BRICKS, dtype=jnp.int32) % BRK_DEV
    edge = (position == 0) | (position == BRK_DEV - 1)
    return jnp.where(edge | (pick < 3), 1, 0).astype(jnp.int32)


def level_of(rng, dims, pieces, least, high):
    def one(dim, blocks):
        steps = jax.random.uniform(jax.random.fold_in(jax.random.fold_in(rng, 6), dim), (blocks,), jnp.float32, least / len(pieces), high / len(pieces))
        return jnp.repeat(jnp.exp(steps), dims[dim] // blocks).reshape((-1,) + (1,) * (len(dims) - dim - 1))

    factor_of = one(*pieces[0])
    for cut in pieces[1:]:
        factor_of = factor_of * one(*cut)
    return factor_of


def setup_inputs(seed: int = 0) -> dict:
    key_of = jax.random.split(jax.random.key(seed), 5)
    return {
        "image": draw_image(jax.random.fold_in(key_of[4], 71), 0),
        "shifts": draw_shifts(jax.random.fold_in(key_of[4], 71), 0),
        "fractions": jnp.clip(1.0 * jax.random.uniform(key_of[2], (ROUNDS, BRICKS), jnp.float32) ** level_of(key_of[2], (ROUNDS, BRICKS), ((0, 8), (1, 64)), -0.2, 0.2), 0.0, 1.0),
        "valid": draw_valid(jax.random.fold_in(key_of[4], 71), 0),
    }


sigma_spot = 1.5

def kernel_tables(count):
    index = jnp.arange(count, dtype=jnp.float32)
    offset = index[:, None] - index[None, :]
    smooth = jnp.exp(-offset * offset / (2.0 * sigma_spot * sigma_spot)) / (2.5066282746310002 * sigma_spot)
    smooth = jnp.where(jnp.abs(offset) < 4.0 * sigma_spot, smooth, jnp.float32(0.0))
    curve = (offset * offset / sigma_spot ** 4 - 1.0 / sigma_spot ** 2) * smooth
    return (smooth, curve)

def spot_filter(field):
    values = field.astype(jnp.float32)
    depth, height, width = field.shape[-3:]
    gauss_z, curve_z = kernel_tables(depth)
    gauss_y, curve_y = kernel_tables(height)
    gauss_x, curve_x = kernel_tables(width)
    high = lax.Precision.HIGHEST
    along_x = jnp.einsum('...x,wx->...w', values, gauss_x, precision=high)
    bent_x = jnp.einsum('...x,wx->...w', values, curve_x, precision=high)
    plain_y = jnp.einsum('...yx,vy->...vx', along_x, gauss_y, precision=high)
    bent_y = jnp.einsum('...yx,vy->...vx', along_x, curve_y, precision=high)
    mixed_y = jnp.einsum('...yx,vy->...vx', bent_x, gauss_y, precision=high)
    outer = jnp.einsum('...zyx,wz->...wyx', mixed_y + bent_y, gauss_z, precision=high)
    outer = outer + jnp.einsum('...zyx,wz->...wyx', plain_y, curve_z, precision=high)
    return (-(sigma_spot * sigma_spot) * outer).astype(jnp.bfloat16)

def shift_strip(padded, offsets, fraction_row, width):

    def one_brick(start, fraction):
        window = lax.dynamic_slice_in_dim(padded, start, width + 1, padded.ndim - 1).astype(jnp.float32)
        return ((1.0 - fraction) * window[..., 1:] + fraction * window[..., :-1]).astype(jnp.bfloat16)
    return jax.vmap(one_brick)(offsets, fraction_row)

def reference(image, shifts, fractions, valid):
    depth, height, width = image.shape[-3:]
    bricks = image.shape[1]
    reach = SMAX + 1
    weights = valid.astype(jnp.bfloat16)
    masked = image * weights[None, :, None, None, None, None]

    def per_round(items):
        layer, shift_row, fraction_row = items
        strip = jnp.moveaxis(layer, 0, 3).reshape(layer.shape[1], depth, height, bricks * width)
        padded = jnp.pad(strip, ((0, 0), (0, 0), (0, 0), (reach, reach)))
        offsets = (jnp.arange(bricks, dtype=jnp.int32) * width + reach - shift_row - 1).astype(jnp.int32)
        shifted = shift_strip(padded, offsets, fraction_row, width)
        filtered = spot_filter(shifted)
        magnitude = lax.optimization_barrier(jnp.sum(jnp.abs(filtered.astype(jnp.float32)), axis=(2, 3, 4)))
        total = lax.optimization_barrier(jnp.sum(magnitude * valid.astype(jnp.float32)[:, None], axis=0))
        return (filtered, total)
    filtered, total = lax.map(per_round, (masked, shifts, fractions))
    count = jnp.maximum(jnp.sum(valid).astype(jnp.float32), 1.0)
    scale = total / (count * depth * height * width) + 1e-06

    def per_brick(block):
        ratio = block.astype(jnp.float32) / scale[:, :, None, None, None]
        energy = lax.optimization_barrier(jnp.mean(ratio * ratio, axis=(0, 1), keepdims=True))
        return (ratio / jnp.sqrt(energy + 1.0)).astype(jnp.bfloat16)
    normed = lax.map(per_brick, jnp.moveaxis(filtered, 1, 0))
    rounds = image.shape[0]
    quarter = BRK_DEV // N_ROUND
    tail = normed.shape[2:]
    arranged = normed.reshape((N_BRICK, N_ROUND, quarter, rounds) + tail)
    arranged = jnp.transpose(arranged, (3, 1, 0, 2, 4, 5, 6, 7))
    return arranged.reshape((rounds, N_ROUND, N_BRICK * quarter) + tail)
```

```python
import functools
import math

import jax
import jax.numpy as jnp
import ml_dtypes
import numpy as np
from jax import lax
from jax.experimental import pallas as pl
from jax.experimental.pallas import tpu as pltpu
from jax.sharding import PartitionSpec as P

MESH = pl.DeviceIdType.MESH
SIGMA = 1.5
HALO = 32
BF16 = jnp.bfloat16
F32 = jnp.float32


def tables(count):
    index = np.arange(count, dtype=np.float64)
    offset = index[:, None] - index[None, :]
    smooth = np.exp(-offset * offset / (2.0 * SIGMA * SIGMA)) / (math.sqrt(2.0 * math.pi) * SIGMA)
    smooth = np.where(np.abs(offset) < 4.0 * SIGMA, smooth, 0.0)
    curve = (offset * offset / SIGMA**4 - 1.0 / SIGMA**2) * smooth
    return smooth, curve


def split(matrix):
    high = matrix.astype(ml_dtypes.bfloat16)
    low = (matrix - high.astype(np.float64)).astype(ml_dtypes.bfloat16)
    return high, low


def weights(depth, height, width):
    gz, sz = tables(depth)
    gy, sy = tables(height)
    gx, sx = tables(width)
    plain = np.kron(gz, gy)
    bent = np.kron(gz, sy) + np.kron(sz, gy)
    zy = -(SIGMA * SIGMA) * np.concatenate([plain, bent], axis=0)
    zy = np.concatenate(split(zy), axis=0)
    x = np.concatenate(split(np.concatenate([sx.T, gx.T], axis=0)), axis=1)
    return zy, x


def iota(shape, dim):
    return lax.broadcasted_iota(jnp.int32, shape, dim)


def dot(a, b):
    return jnp.dot(a, b, preferred_element_type=F32)


def kernel(sizes, img, shifts, fractions, valid, counts, w1h, w2h, out, ext, send, recv, halo_out, halo_in,
           w1, w2, diff, shifted, yhi, ylo, acc, tile_a, tile_b, tile_c, recv_a, recv_b, recv_c, inv,
           load_sem, w_sem, send_sem, recv_sem, halo_ssem, halo_rsem, red_ssem, red_rsem):
    rounds, bricks, zs, ys, voxels = sizes
    channels, area, width = ext.shape[1:]
    me = lax.axis_index("round")
    col = lax.axis_index("brick")
    z = lax.rem(col, zs)
    y = col // zs

    def z_peer(d):
        return y * zs + lax.rem(z + d, zs)

    def y_peer(d):
        return lax.rem(y + d, ys) * zs + z

    last = lax.axis_size("brick")
    right, left = lax.rem(col + 1, last), lax.rem(col + last - 1, last)

    barrier = pltpu.get_barrier_semaphore()
    for d in range(1, rounds):
        pl.semaphore_signal(barrier, inc=1, device_id={"round": lax.rem(me + d, rounds)}, device_id_type=MESH)
    for j in [right, left] + [z_peer(d) for d in range(1, zs)] + [y_peer(d) for d in range(1, ys)]:
        pl.semaphore_signal(barrier, inc=1, device_id={"brick": j}, device_id_type=MESH)

    loads = [pltpu.make_async_copy(img.at[k], ext.at[k + 1], load_sem.at[k]) for k in range(bricks)]
    loads += [pltpu.make_async_copy(w1h, w1, w_sem.at[0]), pltpu.make_async_copy(w2h, w2, w_sem.at[1])]
    for c in loads:
        c.start()

    shape = (width, 2 * width)
    lane = iota(shape, 1)
    diff[...] = iota(shape, 0) - (lane & (width - 1)) + (lane >> 7)
    acc[...] = jnp.zeros_like(acc)
    for c in loads:
        c.wait()

    def pack_mask(shape, packed, long, start):
        p, q = iota(shape, packed), iota(shape, long)
        return jnp.where((p >> 5) * width + start + (p & (HALO - 1)) == q, 1.0, 0.0).astype(BF16)

    def flat(k):
        return jnp.concatenate([ext[k, c] for c in range(channels)], axis=1)

    halo_out[0] = dot(flat(bricks), pack_mask((channels * width, width), 1, 0, width - HALO)).astype(BF16)
    halo_out[1] = dot(flat(1), pack_mask((channels * width, width), 1, 0, 0)).astype(BF16)
    pl.semaphore_wait(barrier, rounds - 1 + 2 + zs - 1 + ys - 1)

    halos = [
        pltpu.make_async_remote_copy(
            src_ref=halo_out.at[i], dst_ref=halo_in.at[i], send_sem=halo_ssem.at[i], recv_sem=halo_rsem.at[i],
            device_id={"brick": j}, device_id_type=MESH)
        for i, j in ((0, right), (1, left))
    ]
    for c in halos:
        c.start()

    def unpack_halos():
        for i, (slot, start) in enumerate(((0, width - HALO), (bricks + 1, 0))):
            halos[i].wait_recv()
            wide = dot(halo_in[i], pack_mask((width, channels * width), 0, 1, start)).astype(BF16)
            for c in range(channels):
                ext[slot, c] = wide[:, c * width:(c + 1) * width]

    chip, core = me // 2, lax.rem(me, 2)
    chips = rounds // 2

    def brick_of(step):
        turn = lax.rem(step, 3)
        late = step // 3
        ahead = jnp.where(turn == 2, 2, jnp.where(turn == core, 1, chips - 1))
        there = lax.rem(chip + ahead, chips)
        first = jnp.where(there < chips // 2, 1, 0)
        far = 2 * there + jnp.where(late == 0, first, 1 - first)
        return jnp.where(step < 6, far, jnp.where(step == 6, 2 * chip + 1 - core, me))

    def bulk(k):
        return pltpu.make_async_remote_copy(
            src_ref=send.at[k], dst_ref=recv.at[me], send_sem=send_sem.at[k], recv_sem=recv_sem.at[me],
            device_id={"round": k}, device_id_type=MESH)

    def filter_brick(k):
        s = shifts[0, k]
        f = fractions[0, k]
        here = col * bricks + k
        v_left = jnp.where(here > 0, valid[jnp.maximum(here - 1, 0)], 0)
        v_right = jnp.where(here < last * bricks - 1, valid[jnp.minimum(here + 1, last * bricks - 1)], 0)
        v_here = valid[here].astype(F32)
        v_next = jnp.where(s >= 0, v_left, v_right).astype(F32)
        t_next = jnp.where(s >= 0, width, -width) - s
        pick = jnp.concatenate([
            jnp.where(diff[...] == -s, v_here, 0.0).astype(BF16),
            jnp.where(diff[...] == t_next, v_next, 0.0).astype(BF16)], axis=0)
        flat_rows = (channels * area, width)
        is_left = jnp.where(s >= 0, 1.0, 0.0).astype(BF16)
        is_right = jnp.where(s >= 0, 0.0, 1.0).astype(BF16)
        beside = ext[k].reshape(flat_rows) * is_left + ext[k + 2].reshape(flat_rows) * is_right
        moved = dot(jnp.concatenate([ext[k + 1].reshape(flat_rows), beside], axis=1), pick)
        shifted[...] = ((1.0 - f) * moved[:, :width] + f * moved[:, width:]).astype(BF16)
        field = jnp.concatenate([shifted[c * area:(c + 1) * area] for c in range(channels)], axis=1)
        planes = dot(w1[:2 * area], field) + dot(w1[2 * area:], field)
        for c in range(channels):
            both = jnp.concatenate([
                planes[:area, c * width:(c + 1) * width], planes[area:, c * width:(c + 1) * width]], axis=1)
            high = both.astype(BF16)
            yhi[c * area:(c + 1) * area] = high
            ylo[c * area:(c + 1) * area] = (both - high.astype(F32)).astype(BF16)
        twice = dot(yhi[...], w2[...])
        result = (twice[:, :width] + twice[:, width:] + dot(ylo[...], w2[:, :width])).astype(BF16)
        send[k] = result.reshape(channels, area, width)
        size = jnp.abs(result.astype(F32)).reshape(channels, area // 8, 8, width)
        acc[...] += jnp.sum(size, axis=1) * v_here

    def step_body(step, _):
        @pl.when(step == 3)
        def _():
            unpack_halos()

        k = brick_of(step)
        filter_brick(k)

        @pl.when(step < rounds - 1)
        def _():
            bulk(k).start()

        return 0

    lax.fori_loop(0, rounds, step_body, 0)
    recv[me] = send[me]

    def gather(tile, slots, peers, index):
        copies = [
            pltpu.make_async_remote_copy(
                src_ref=tile, dst_ref=slots.at[d], send_sem=red_ssem.at[index], recv_sem=red_rsem.at[index],
                device_id=peer, device_id_type=MESH)
            for d, peer in enumerate(peers)
        ]
        for c in copies:
            c.start()
        pltpu.make_async_copy(slots, slots, red_rsem.at[index]).wait()
        return tile[...] + jnp.sum(slots[...], axis=0)

    tile_a[...] = jnp.zeros_like(tile_a)
    tile_a[:channels] = jnp.sum(acc[...], axis=1)
    tile_b[...] = gather(tile_a, recv_a, [{"brick": z_peer(d)} for d in range(1, zs)], 0)
    tile_c[...] = gather(tile_b, recv_b, [{"brick": y_peer(d)} for d in range(1, ys)], 1)
    totals = [
        pltpu.make_async_remote_copy(
            src_ref=tile_c, dst_ref=recv_c.at[me], send_sem=red_ssem.at[2], recv_sem=red_rsem.at[2],
            device_id={"round": lax.rem(me + d, rounds)}, device_id_type=MESH)
        for d in range(1, rounds)
    ]
    for c in totals:
        c.start()
    seven = recv_c.at[pl.ds(0, rounds - 1)]
    pltpu.make_async_copy(seven, seven, red_rsem.at[2]).wait()
    recv_c[me] = tile_c[...]
    count = jnp.maximum(jnp.sum(counts[...].astype(F32)), 1.0)
    total = jnp.sum(recv_c[...], axis=2, keepdims=True)
    inv[...] = jnp.broadcast_to(1.0 / (total / (count * voxels) + 1e-06), inv.shape)

    for d in range(1, rounds):
        source = lax.rem(me + d, rounds)
        pltpu.make_async_copy(recv.at[source], recv.at[source], recv_sem.at[source]).wait()

    def norm_body(i, _):
        rows = pl.ds(pl.multiple_of(i * 16, 16), 16)
        energy = jnp.zeros((16, width), F32)
        for r in range(rounds):
            for c in range(channels):
                a = recv[r, c, rows].astype(F32) * inv[r, c:c + 1]
                energy += a * a
        root = lax.rsqrt(energy * (1.0 / (rounds * channels)) + 1.0)
        for r in range(rounds):
            for c in range(channels):
                a = recv[r, c, rows].astype(F32) * inv[r, c:c + 1]
                out[r, c, rows] = (a * root).astype(BF16)
        return 0

    lax.fori_loop(0, area // 16, norm_body, 0)

    for c in halos:
        c.wait_send()
    for d in range(1, rounds):
        k = lax.rem(me + d, rounds)
        bulk(k).wait_send()
    pltpu.make_async_copy(recv_a, recv_a, red_ssem.at[0]).wait()
    pltpu.make_async_copy(recv_b, recv_b, red_ssem.at[1]).wait()
    pltpu.make_async_copy(seven, seven, red_ssem.at[2]).wait()


def on_device(image, shifts, fractions, valid):
    _, bricks, channels, depth, height, width = image.shape
    rounds = lax.axis_size("round")
    zs, ys = 16, 4
    area = depth * height
    w1, w2 = weights(depth, height, width)
    anywhere = pl.BlockSpec(memory_space=pl.ANY)
    scalars = pl.BlockSpec(memory_space=pltpu.SMEM)
    vector = pl.BlockSpec(memory_space=pltpu.VMEM)
    tile = (8, width)
    sems = pltpu.SemaphoreType.DMA
    out = pl.pallas_call(
        functools.partial(kernel, (rounds, bricks, zs, ys, depth * height * width)),
        out_shape=jax.ShapeDtypeStruct((rounds, channels, area, width), BF16),
        in_specs=[anywhere, scalars, scalars, scalars, vector, anywhere, anywhere],
        out_specs=vector,
        scratch_shapes=[
            pltpu.VMEM((bricks + 2, channels, area, width), BF16),
            pltpu.VMEM((bricks, channels, area, width), BF16),
            pltpu.VMEM((rounds, channels, area, width), BF16),
            pltpu.VMEM((2, area, width), BF16),
            pltpu.VMEM((2, area, width), BF16),
            pltpu.VMEM(w1.shape, BF16),
            pltpu.VMEM(w2.shape, BF16),
            pltpu.VMEM((width, 2 * width), jnp.int32),
            pltpu.VMEM((channels * area, width), BF16),
            pltpu.VMEM((channels * area, 2 * width), BF16),
            pltpu.VMEM((channels * area, 2 * width), BF16),
            pltpu.VMEM((channels,) + tile, F32),
            pltpu.VMEM(tile, F32),
            pltpu.VMEM(tile, F32),
            pltpu.VMEM(tile, F32),
            pltpu.VMEM((zs - 1,) + tile, F32),
            pltpu.VMEM((ys - 1,) + tile, F32),
            pltpu.VMEM((rounds,) + tile, F32),
            pltpu.VMEM((rounds,) + tile, F32),
            sems((bricks,)), sems((2,)), sems((bricks,)), sems((rounds,)), sems((2,)), sems((2,)), sems((3,)),
            sems((3,)),
        ],
        compiler_params=pltpu.CompilerParams(
            collective_id=0, has_side_effects=True, vmem_limit_bytes=48 * 2**20),
        name="spots",
    )(image.reshape(bricks, channels, area, width), shifts, fractions, valid, valid.reshape(-1, width),
      jnp.asarray(w1), jnp.asarray(w2))
    return out.reshape(rounds, 1, 1, channels, depth, height, width)


def solution(mesh):
    return jax.shard_map(
        on_device,
        mesh=mesh,
        in_specs=(P("round", "brick"), P("round", "brick"), P("round", "brick"), P()),
        out_specs=P(None, "round", "brick"),
        check_vma=False,
    )
```

```python
import functools
import math

import jax
import jax.numpy as jnp
import ml_dtypes
import numpy as np
from jax import lax
from jax.experimental import pallas as pl
from jax.experimental.pallas import tpu as pltpu
from jax.sharding import PartitionSpec as P

MESH = pl.DeviceIdType.MESH
SIGMA = 1.5
HALO = 32
BF16 = jnp.bfloat16
F32 = jnp.float32


def tables(count):
    index = np.arange(count, dtype=np.float64)
    offset = index[:, None] - index[None, :]
    smooth = np.exp(-offset * offset / (2.0 * SIGMA * SIGMA)) / (math.sqrt(2.0 * math.pi) * SIGMA)
    smooth = np.where(np.abs(offset) < 4.0 * SIGMA, smooth, 0.0)
    curve = (offset * offset / SIGMA**4 - 1.0 / SIGMA**2) * smooth
    return smooth, curve


def split(matrix):
    high = matrix.astype(ml_dtypes.bfloat16)
    low = (matrix - high.astype(np.float64)).astype(ml_dtypes.bfloat16)
    return high, low


def weights(depth, height, width):
    gz, sz = tables(depth)
    gy, sy = tables(height)
    gx, sx = tables(width)
    plain = np.kron(gz, gy)
    bent = np.kron(gz, sy) + np.kron(sz, gy)
    zy = -(SIGMA * SIGMA) * np.concatenate([plain, bent], axis=0)
    zy = np.concatenate(split(zy), axis=0)
    x = np.concatenate(split(np.concatenate([sx.T, gx.T], axis=0)), axis=1)
    return zy, x


def iota(shape, dim):
    return lax.broadcasted_iota(jnp.int32, shape, dim)


def dot(a, b):
    return jnp.dot(a, b, preferred_element_type=F32)


def kernel(sizes, img, shifts_h, fractions_h, valid_h, counts_h, w1h, w2h, out, shifts, fractions, valid, counts, ext, send, recv, halo_out, halo_in,
           w1, w2, diff, shifted, yhi, ylo, acc, row_a, row_b, recv_a, recv_b, inv,
           load_sem, w_sem, send_sem, recv_sem, halo_ssem, halo_rsem, red_ssem, red_rsem):
    rounds, bricks, zs, ys, voxels = sizes
    channels, area, width = ext.shape[1:]
    me = lax.axis_index("round")
    col = lax.axis_index("brick")
    z = lax.rem(col, zs)
    y = col // zs

    last = lax.axis_size("brick")
    right, left = lax.rem(col + 1, last), lax.rem(col + last - 1, last)

    loads = [pltpu.make_async_copy(img.at[k], ext.at[k + 1], load_sem.at[k]) for k in range(bricks)]
    small = ((shifts_h, shifts), (fractions_h, fractions), (valid_h, valid), (w1h, w1), (w2h, w2), (counts_h, counts))
    loads = [pltpu.make_async_copy(a, b, w_sem.at[i]) for i, (a, b) in enumerate(small)] + loads
    for c in loads:
        c.start()

    line = [{"brick": y * zs + lax.rem(z + d, zs)} for d in range(1, zs)]
    plane = [
        {"round": lax.rem(me + a, rounds), "brick": lax.rem(y + b, ys) * zs + z}
        for b in range(ys) for a in range(rounds) if a or b]
    barrier = pltpu.get_barrier_semaphore()
    for peer in [{"brick": right}, {"brick": left}] + line + plane:
        pl.semaphore_signal(barrier, inc=1, device_id=peer, device_id_type=MESH)

    shape = (width, 2 * width)
    lane = iota(shape, 1)
    diff[...] = iota(shape, 0) - (lane & (width - 1)) + (lane >> 7)
    acc[...] = jnp.zeros_like(acc)
    for c in loads:
        c.wait()

    def pack_mask(shape, packed, long, start):
        p, q = iota(shape, packed), iota(shape, long)
        return jnp.where((p >> 5) * width + start + (p & (HALO - 1)) == q, 1.0, 0.0).astype(BF16)

    def flat(k):
        return jnp.concatenate([ext[k, c] for c in range(channels)], axis=1)

    halo_out[0] = dot(flat(bricks), pack_mask((channels * width, width), 1, 0, width - HALO)).astype(BF16)
    halo_out[1] = dot(flat(1), pack_mask((channels * width, width), 1, 0, 0)).astype(BF16)
    pl.semaphore_wait(barrier, 2 + len(line) + len(plane))

    halos = [
        pltpu.make_async_remote_copy(
            src_ref=halo_out.at[i], dst_ref=halo_in.at[i], send_sem=halo_ssem.at[i], recv_sem=halo_rsem.at[i],
            device_id={"brick": j}, device_id_type=MESH)
        for i, j in ((0, right), (1, left))
    ]
    for c in halos:
        c.start()

    def unpack_halos():
        for i, (slot, start) in enumerate(((0, width - HALO), (bricks + 1, 0))):
            halos[i].wait_recv()
            wide = dot(halo_in[i], pack_mask((width, channels * width), 0, 1, start)).astype(BF16)
            for c in range(channels):
                ext[slot, c] = wide[:, c * width:(c + 1) * width]

    chip, core = me // 2, lax.rem(me, 2)
    chips = rounds // 2

    def brick_of(step):
        turn = lax.rem(step, 3)
        late = step // 3
        ahead = jnp.where(turn == 2, 2, jnp.where(turn == core, 1, chips - 1))
        there = lax.rem(chip + ahead, chips)
        first = jnp.where(there < chips // 2, 1, 0)
        far = 2 * there + jnp.where(late == 0, first, 1 - first)
        return jnp.where(step < 6, far, jnp.where(step == 6, 2 * chip + 1 - core, me))

    def bulk(k):
        return pltpu.make_async_remote_copy(
            src_ref=send.at[k], dst_ref=recv.at[me], send_sem=send_sem.at[k], recv_sem=recv_sem.at[me],
            device_id={"round": k}, device_id_type=MESH)

    def filter_brick(k):
        s = shifts[0, k]
        f = fractions[0, k]
        here = col * bricks + k
        v_left = jnp.where(here > 0, valid[jnp.maximum(here - 1, 0)], 0)
        v_right = jnp.where(here < last * bricks - 1, valid[jnp.minimum(here + 1, last * bricks - 1)], 0)
        v_here = valid[here].astype(F32)
        v_next = jnp.where(s >= 0, v_left, v_right).astype(F32)
        t_next = jnp.where(s >= 0, width, -width) - s
        pick = jnp.concatenate([
            jnp.where(diff[...] == -s, v_here, 0.0).astype(BF16),
            jnp.where(diff[...] == t_next, v_next, 0.0).astype(BF16)], axis=0)
        flat_rows = (channels * area, width)
        is_left = jnp.where(s >= 0, 1.0, 0.0).astype(BF16)
        is_right = jnp.where(s >= 0, 0.0, 1.0).astype(BF16)
        beside = ext[k].reshape(flat_rows) * is_left + ext[k + 2].reshape(flat_rows) * is_right
        moved = dot(jnp.concatenate([ext[k + 1].reshape(flat_rows), beside], axis=1), pick)
        shifted[...] = ((1.0 - f) * moved[:, :width] + f * moved[:, width:]).astype(BF16)
        field = jnp.concatenate([shifted[c * area:(c + 1) * area] for c in range(channels)], axis=1)
        planes = dot(w1[:2 * area], field) + dot(w1[2 * area:], field)
        for c in range(channels):
            both = jnp.concatenate([
                planes[:area, c * width:(c + 1) * width], planes[area:, c * width:(c + 1) * width]], axis=1)
            high = both.astype(BF16)
            yhi[c * area:(c + 1) * area] = high
            ylo[c * area:(c + 1) * area] = (both - high.astype(F32)).astype(BF16)
        twice = dot(yhi[...], w2[...])
        result = (twice[:, :width] + twice[:, width:] + dot(ylo[...], w2[:, :width])).astype(BF16)
        send[k] = result.reshape(channels, area, width)
        size = jnp.abs(result.astype(F32)).reshape(channels, area // 8, 8, width)
        acc[...] += jnp.sum(size, axis=1) * v_here

    def step_body(step, _):
        @pl.when(step == 3)
        def _():
            unpack_halos()

        k = brick_of(step)
        filter_brick(k)

        @pl.when(step < rounds - 1)
        def _():
            bulk(k).start()

        return 0

    lax.fori_loop(0, rounds, step_body, 0)
    recv[me] = send[me]

    def spread(row, slots, slot_of, peers, index):
        for d, peer in enumerate(peers):
            pltpu.make_async_remote_copy(
                src_ref=row, dst_ref=slots.at[pl.ds(slot_of(d), 1)], send_sem=red_ssem.at[index],
                recv_sem=red_rsem.at[index], device_id=peer, device_id_type=MESH).start()
        every = slots.at[pl.ds(0, len(peers))]
        pltpu.make_async_copy(every, every, red_rsem.at[index]).wait()

    sums = jnp.sum(jnp.sum(acc[...], axis=1), axis=1, keepdims=True)
    group = iota((1, width), 1) // (width // channels)
    row_a[...] = sum(jnp.where(group == c, sums[c:c + 1], 0.0) for c in range(channels))
    spread(row_a, recv_a, lambda d: d, line, 0)
    row_b[...] = row_a[...] + jnp.sum(recv_a[:len(line)], axis=0, keepdims=True)
    spread(row_b, recv_b, lambda d: (d + 1) // rounds * rounds + me, plane, 1)
    recv_b[pl.ds(me, 1)] = row_b[...]
    count = jnp.maximum(jnp.sum(counts[...].astype(F32)), 1.0)
    total = jnp.sum(recv_b[...].reshape(ys, rounds, width), axis=0)
    scale = 1.0 / (total / (count * voxels) + 1e-06)
    for c in range(channels):
        lane = c * (width // channels)
        inv[c] = jnp.broadcast_to(scale[:, lane:lane + 1], (rounds, width))

    for d in range(1, rounds):
        source = lax.rem(me + d, rounds)
        pltpu.make_async_copy(recv.at[source], recv.at[source], recv_sem.at[source]).wait()

    def norm_body(i, _):
        rows = pl.ds(pl.multiple_of(i * 16, 16), 16)
        energy = jnp.zeros((16, width), F32)
        for r in range(rounds):
            for c in range(channels):
                a = recv[r, c, rows].astype(F32) * inv[c, r:r + 1]
                energy += a * a
        root = lax.rsqrt(energy * (1.0 / (rounds * channels)) + 1.0)
        for r in range(rounds):
            for c in range(channels):
                a = recv[r, c, rows].astype(F32) * inv[c, r:r + 1]
                out[r, c, rows] = (a * root).astype(BF16)
        return 0

    lax.fori_loop(0, area // 16, norm_body, 0)

    for c in halos:
        c.wait_send()
    for d in range(1, rounds):
        k = lax.rem(me + d, rounds)
        bulk(k).wait_send()
    for index, (slots, peers) in enumerate(((recv_a, line), (recv_b, plane))):
        every = slots.at[pl.ds(0, len(peers))]
        pltpu.make_async_copy(every, every, red_ssem.at[index]).wait()


def on_device(image, shifts, fractions, valid):
    _, bricks, channels, depth, height, width = image.shape
    rounds = lax.axis_size("round")
    zs, ys = 16, 4
    area = depth * height
    w1, w2 = weights(depth, height, width)
    remote = pl.BlockSpec(memory_space=pltpu.HBM)
    vector = pl.BlockSpec(memory_space=pltpu.VMEM)
    tile = (8, width)
    sems = pltpu.SemaphoreType.DMA
    out = pl.pallas_call(
        functools.partial(kernel, (rounds, bricks, zs, ys, depth * height * width)),
        out_shape=jax.ShapeDtypeStruct((rounds, channels, area, width), BF16),
        in_specs=[remote] * 7,
        out_specs=vector,
        scratch_shapes=[
            pltpu.SMEM(shifts.shape, jnp.int32),
            pltpu.SMEM(fractions.shape, F32),
            pltpu.SMEM(valid.shape, jnp.int32),
            pltpu.VMEM((valid.size // width, width), jnp.int32),
            pltpu.VMEM((bricks + 2, channels, area, width), BF16),
            pltpu.VMEM((bricks, channels, area, width), BF16),
            pltpu.VMEM((rounds, channels, area, width), BF16),
            pltpu.VMEM((2, area, width), BF16),
            pltpu.VMEM((2, area, width), BF16),
            pltpu.VMEM(w1.shape, BF16),
            pltpu.VMEM(w2.shape, BF16),
            pltpu.VMEM((width, 2 * width), jnp.int32),
            pltpu.VMEM((channels * area, width), BF16),
            pltpu.VMEM((channels * area, 2 * width), BF16),
            pltpu.VMEM((channels * area, 2 * width), BF16),
            pltpu.VMEM((channels,) + tile, F32),
            pltpu.VMEM((1, width), F32),
            pltpu.VMEM((1, width), F32),
            pltpu.VMEM((zs, width), F32),
            pltpu.VMEM((ys * rounds, width), F32),
            pltpu.VMEM((channels, rounds, width), F32),
            sems((bricks,)), sems((6,)), sems((bricks,)), sems((rounds,)), sems((2,)), sems((2,)), sems((2,)),
            sems((2,)),
        ],
        compiler_params=pltpu.CompilerParams(
            collective_id=0, has_side_effects=True, vmem_limit_bytes=48 * 2**20),
        name="spots",
    )(*[pltpu.with_memory_space_constraint(a, pltpu.HBM) for a in (
        image.reshape(bricks, channels, area, width), shifts, fractions, valid, valid.reshape(-1, width),
        jnp.asarray(w1), jnp.asarray(w2))])
    return out.reshape(rounds, 1, 1, channels, depth, height, width)


def solution(mesh):
    return jax.shard_map(
        on_device,
        mesh=mesh,
        in_specs=(P("round", "brick"), P("round", "brick"), P("round", "brick"), P()),
        out_specs=P(None, "round", "brick"),
        check_vma=False,
    )
```

```python
import functools
import math

import jax
import jax.numpy as jnp
import ml_dtypes
import numpy as np
from jax import lax
from jax.experimental import pallas as pl
from jax.experimental.pallas import tpu as pltpu
from jax.sharding import PartitionSpec as P

MESH = pl.DeviceIdType.MESH
SIGMA = 1.5
HALO = 32
BF16 = jnp.bfloat16
F32 = jnp.float32


def tables(count):
    index = np.arange(count, dtype=np.float64)
    offset = index[:, None] - index[None, :]
    smooth = np.exp(-offset * offset / (2.0 * SIGMA * SIGMA)) / (math.sqrt(2.0 * math.pi) * SIGMA)
    smooth = np.where(np.abs(offset) < 4.0 * SIGMA, smooth, 0.0)
    curve = (offset * offset / SIGMA**4 - 1.0 / SIGMA**2) * smooth
    return smooth, curve


def split(matrix):
    high = matrix.astype(ml_dtypes.bfloat16)
    low = (matrix - high.astype(np.float64)).astype(ml_dtypes.bfloat16)
    return high, low


def weights(depth, height, width):
    gz, sz = tables(depth)
    gy, sy = tables(height)
    gx, sx = tables(width)
    plain = np.kron(gz, gy)
    bent = np.kron(gz, sy) + np.kron(sz, gy)
    zy = -(SIGMA * SIGMA) * np.concatenate([plain, bent], axis=0)
    zy = np.concatenate(split(zy), axis=0)
    x = np.concatenate(split(np.concatenate([sx.T, gx.T], axis=0)), axis=1)
    return zy, x


def iota(shape, dim):
    return lax.broadcasted_iota(jnp.int32, shape, dim)


def dot(a, b):
    return jnp.dot(a, b, preferred_element_type=F32)


def kernel(sizes, img, shifts_h, fractions_h, valid_h, counts_h, w1h, w2h, out, shifts, fractions, valid, counts, ext, send, recv, halo_out, halo_in,
           w1, w2, diff, shifted, yhi, ylo, acc, row_a, row_b, recv_a, recv_b, inv,
           load_sem, w_sem, send_sem, recv_sem, halo_ssem, halo_rsem, red_ssem, red_rsem):
    rounds, bricks, zs, ys, voxels = sizes
    channels, area, width = ext.shape[1:]
    me = lax.axis_index("round")
    col = lax.axis_index("brick")
    z = lax.rem(col, zs)
    y = col // zs

    last = lax.axis_size("brick")
    right, left = lax.rem(col + 1, last), lax.rem(col + last - 1, last)

    loads = [pltpu.make_async_copy(img.at[k], ext.at[k + 1], load_sem.at[k]) for k in range(bricks)]
    small = ((shifts_h, shifts), (fractions_h, fractions), (valid_h, valid), (w1h, w1), (w2h, w2), (counts_h, counts))
    loads = [pltpu.make_async_copy(a, b, w_sem.at[i]) for i, (a, b) in enumerate(small)] + loads
    for c in loads:
        c.start()

    line = [{"brick": y * zs + lax.rem(z + d, zs)} for d in range(1, zs)]
    plane = [
        {"round": lax.rem(me + a, rounds), "brick": lax.rem(y + b, ys) * zs + z}
        for b in range(ys) for a in range(rounds) if a or b]
    barrier = pltpu.get_barrier_semaphore()
    for peer in [{"brick": right}, {"brick": left}] + line + plane:
        pl.semaphore_signal(barrier, inc=1, device_id=peer, device_id_type=MESH)

    shape = (width, 2 * width)
    lane = iota(shape, 1)
    diff[...] = iota(shape, 0) - (lane & (width - 1)) + (lane >> 7)
    acc[...] = jnp.zeros_like(acc)
    for c in loads:
        c.wait()

    def pack_mask(shape, packed, long, start):
        p, q = iota(shape, packed), iota(shape, long)
        return jnp.where((p >> 5) * width + start + (p & (HALO - 1)) == q, 1.0, 0.0).astype(BF16)

    def flat(k):
        return jnp.concatenate([ext[k, c] for c in range(channels)], axis=1)

    halo_out[0] = dot(flat(bricks), pack_mask((channels * width, width), 1, 0, width - HALO)).astype(BF16)
    halo_out[1] = dot(flat(1), pack_mask((channels * width, width), 1, 0, 0)).astype(BF16)
    pl.semaphore_wait(barrier, 2 + len(line) + len(plane))

    halos = [
        pltpu.make_async_remote_copy(
            src_ref=halo_out.at[i], dst_ref=halo_in.at[i], send_sem=halo_ssem.at[i], recv_sem=halo_rsem.at[i],
            device_id={"brick": j}, device_id_type=MESH)
        for i, j in ((0, right), (1, left))
    ]
    for c in halos:
        c.start()

    def unpack_halos():
        for i, (slot, start) in enumerate(((0, width - HALO), (bricks + 1, 0))):
            halos[i].wait_recv()
            wide = dot(halo_in[i], pack_mask((width, channels * width), 0, 1, start)).astype(BF16)
            for c in range(channels):
                ext[slot, c] = wide[:, c * width:(c + 1) * width]

    chip, core = me // 2, lax.rem(me, 2)
    chips = rounds // 2

    def brick_of(step):
        turn = lax.rem(step, 3)
        late = step // 3
        ahead = jnp.where(turn == 2, 2, jnp.where(turn == core, 1, chips - 1))
        there = lax.rem(chip + ahead, chips)
        first = jnp.where(there < chips // 2, 1, 0)
        far = 2 * there + jnp.where(late == 0, first, 1 - first)
        return jnp.where(step < 6, far, jnp.where(step == 6, 2 * chip + 1 - core, me))

    groups = ((0, area // 2), (area // 2, area // 4), (3 * area // 4, area // 4))

    def bulk(k, g):
        rows = pl.ds(*groups[g])
        return pltpu.make_async_remote_copy(
            src_ref=send.at[k, :, rows], dst_ref=recv.at[me, :, rows], send_sem=send_sem.at[k, g],
            recv_sem=recv_sem.at[me, g], device_id={"round": k}, device_id_type=MESH)

    def filter_brick(k):
        s = shifts[0, k]
        f = fractions[0, k]
        here = col * bricks + k
        v_left = jnp.where(here > 0, valid[jnp.maximum(here - 1, 0)], 0)
        v_right = jnp.where(here < last * bricks - 1, valid[jnp.minimum(here + 1, last * bricks - 1)], 0)
        v_here = valid[here].astype(F32)
        v_next = jnp.where(s >= 0, v_left, v_right).astype(F32)
        t_next = jnp.where(s >= 0, width, -width) - s
        pick = jnp.concatenate([
            jnp.where(diff[...] == -s, v_here, 0.0).astype(BF16),
            jnp.where(diff[...] == t_next, v_next, 0.0).astype(BF16)], axis=0)
        flat_rows = (channels * area, width)
        is_left = jnp.where(s >= 0, 1.0, 0.0).astype(BF16)
        is_right = jnp.where(s >= 0, 0.0, 1.0).astype(BF16)
        beside = ext[k].reshape(flat_rows) * is_left + ext[k + 2].reshape(flat_rows) * is_right
        moved = dot(jnp.concatenate([ext[k + 1].reshape(flat_rows), beside], axis=1), pick)
        shifted[...] = ((1.0 - f) * moved[:, :width] + f * moved[:, width:]).astype(BF16)
        field = jnp.concatenate([shifted[c * area:(c + 1) * area] for c in range(channels)], axis=1)
        planes = dot(w1[:2 * area], field) + dot(w1[2 * area:], field)
        for c in range(channels):
            both = jnp.concatenate([
                planes[:area, c * width:(c + 1) * width], planes[area:, c * width:(c + 1) * width]], axis=1)
            high = both.astype(BF16)
            yhi[c * area:(c + 1) * area] = high
            ylo[c * area:(c + 1) * area] = (both - high.astype(F32)).astype(BF16)
        twice = dot(yhi[...], w2[...])
        result = (twice[:, :width] + twice[:, width:] + dot(ylo[...], w2[:, :width])).astype(BF16)
        send[k] = result.reshape(channels, area, width)
        size = jnp.abs(result.astype(F32)).reshape(channels, area // 8, 8, width)
        acc[...] += jnp.sum(size, axis=1) * v_here

    def step_body(step, _):
        @pl.when(step == 3)
        def _():
            unpack_halos()

        k = brick_of(step)
        filter_brick(k)

        @pl.when(step < rounds - 1)
        def _():
            bulk(k, 0).start()

        return 0

    lax.fori_loop(0, rounds, step_body, 0)

    def spread(row, slots, slot_of, peers, index):
        for d, peer in enumerate(peers):
            pltpu.make_async_remote_copy(
                src_ref=row, dst_ref=slots.at[pl.ds(slot_of(d), 1)], send_sem=red_ssem.at[index],
                recv_sem=red_rsem.at[index], device_id=peer, device_id_type=MESH).start()

    def arrived(slots, peers, index):
        every = slots.at[pl.ds(0, len(peers))]
        pltpu.make_async_copy(every, every, red_rsem.at[index]).wait()

    sums = jnp.sum(jnp.sum(acc[...], axis=1), axis=1, keepdims=True)
    group = iota((1, width), 1) // (width // channels)
    row_a[...] = sum(jnp.where(group == c, sums[c:c + 1], 0.0) for c in range(channels))
    spread(row_a, recv_a, lambda d: d, line, 0)
    later = [(step, g) for g in (1, 2) for step in [rounds - 2] + list(range(rounds - 2))]
    held = rounds - 1 + 3
    for step, g in later[:held]:
        bulk(brick_of(step), g).start()
    recv[me] = send[me]
    arrived(recv_a, line, 0)
    row_b[...] = row_a[...] + jnp.sum(recv_a[:len(line)], axis=0, keepdims=True)
    spread(row_b, recv_b, lambda d: (d + 1) // rounds * rounds + me, plane, 1)
    for step, g in later[held:]:
        bulk(brick_of(step), g).start()
    arrived(recv_b, plane, 1)
    recv_b[pl.ds(me, 1)] = row_b[...]
    count = jnp.maximum(jnp.sum(counts[...].astype(F32)), 1.0)
    total = jnp.sum(recv_b[...].reshape(ys, rounds, width), axis=0)
    scale = 1.0 / (total / (count * voxels) + 1e-06)
    for c in range(channels):
        lane = c * (width // channels)
        inv[c] = jnp.broadcast_to(scale[:, lane:lane + 1], (rounds, width))

    def norm_body(i, _):
        rows = pl.ds(pl.multiple_of(i * 16, 16), 16)
        energy = jnp.zeros((16, width), F32)
        for r in range(rounds):
            for c in range(channels):
                a = recv[r, c, rows].astype(F32) * inv[c, r:r + 1]
                energy += a * a
        root = lax.rsqrt(energy * (1.0 / (rounds * channels)) + 1.0)
        for r in range(rounds):
            for c in range(channels):
                a = recv[r, c, rows].astype(F32) * inv[c, r:r + 1]
                out[r, c, rows] = (a * root).astype(BF16)
        return 0

    for g, (start, size) in enumerate(groups):
        for d in range(1, rounds):
            source = lax.rem(me + d, rounds)
            piece = recv.at[source, :, pl.ds(start, size)]
            pltpu.make_async_copy(piece, piece, recv_sem.at[source, g]).wait()
        lax.fori_loop(start // 16, (start + size) // 16, norm_body, 0)

    for c in halos:
        c.wait_send()
    for d in range(1, rounds):
        k = lax.rem(me + d, rounds)
        for g in range(len(groups)):
            bulk(k, g).wait_send()
    for index, (slots, peers) in enumerate(((recv_a, line), (recv_b, plane))):
        every = slots.at[pl.ds(0, len(peers))]
        pltpu.make_async_copy(every, every, red_ssem.at[index]).wait()


def on_device(image, shifts, fractions, valid):
    _, bricks, channels, depth, height, width = image.shape
    rounds = lax.axis_size("round")
    zs, ys = 16, 4
    area = depth * height
    w1, w2 = weights(depth, height, width)
    remote = pl.BlockSpec(memory_space=pltpu.HBM)
    vector = pl.BlockSpec(memory_space=pltpu.VMEM)
    tile = (8, width)
    sems = pltpu.SemaphoreType.DMA
    out = pl.pallas_call(
        functools.partial(kernel, (rounds, bricks, zs, ys, depth * height * width)),
        out_shape=jax.ShapeDtypeStruct((rounds, channels, area, width), BF16),
        in_specs=[remote] * 7,
        out_specs=vector,
        scratch_shapes=[
            pltpu.SMEM(shifts.shape, jnp.int32),
            pltpu.SMEM(fractions.shape, F32),
            pltpu.SMEM(valid.shape, jnp.int32),
            pltpu.VMEM((valid.size // width, width), jnp.int32),
            pltpu.VMEM((bricks + 2, channels, area, width), BF16),
            pltpu.VMEM((bricks, channels, area, width), BF16),
            pltpu.VMEM((rounds, channels, area, width), BF16),
            pltpu.VMEM((2, area, width), BF16),
            pltpu.VMEM((2, area, width), BF16),
            pltpu.VMEM(w1.shape, BF16),
            pltpu.VMEM(w2.shape, BF16),
            pltpu.VMEM((width, 2 * width), jnp.int32),
            pltpu.VMEM((channels * area, width), BF16),
            pltpu.VMEM((channels * area, 2 * width), BF16),
            pltpu.VMEM((channels * area, 2 * width), BF16),
            pltpu.VMEM((channels,) + tile, F32),
            pltpu.VMEM((1, width), F32),
            pltpu.VMEM((1, width), F32),
            pltpu.VMEM((zs, width), F32),
            pltpu.VMEM((ys * rounds, width), F32),
            pltpu.VMEM((channels, rounds, width), F32),
            sems((bricks,)), sems((6,)), sems((bricks, 3)), sems((rounds, 3)), sems((2,)), sems((2,)), sems((2,)),
            sems((2,)),
        ],
        compiler_params=pltpu.CompilerParams(
            collective_id=0, has_side_effects=True, vmem_limit_bytes=48 * 2**20),
        name="spots",
    )(*[pltpu.with_memory_space_constraint(a, pltpu.HBM) for a in (
        image.reshape(bricks, channels, area, width), shifts, fractions, valid, valid.reshape(-1, width),
        jnp.asarray(w1), jnp.asarray(w2))])
    return out.reshape(rounds, 1, 1, channels, depth, height, width)


def solution(mesh):
    return jax.shard_map(
        on_device,
        mesh=mesh,
        in_specs=(P("round", "brick"), P("round", "brick"), P("round", "brick"), P()),
        out_specs=P(None, "round", "brick"),
        check_vma=False,
    )
```

```python
import functools
import math

import jax
import jax.numpy as jnp
import ml_dtypes
import numpy as np
from jax import lax
from jax.experimental import pallas as pl
from jax.experimental.pallas import tpu as pltpu
from jax.sharding import PartitionSpec as P

MESH = pl.DeviceIdType.MESH
SIGMA = 1.5
HALO = 32
BF16 = jnp.bfloat16
F32 = jnp.float32


def tables(count):
    index = np.arange(count, dtype=np.float64)
    offset = index[:, None] - index[None, :]
    smooth = np.exp(-offset * offset / (2.0 * SIGMA * SIGMA)) / (math.sqrt(2.0 * math.pi) * SIGMA)
    smooth = np.where(np.abs(offset) < 4.0 * SIGMA, smooth, 0.0)
    curve = (offset * offset / SIGMA**4 - 1.0 / SIGMA**2) * smooth
    return smooth, curve


def split(matrix):
    high = matrix.astype(ml_dtypes.bfloat16)
    low = (matrix - high.astype(np.float64)).astype(ml_dtypes.bfloat16)
    return high, low


def weights(depth, height, width):
    gz, sz = tables(depth)
    gy, sy = tables(height)
    gx, sx = tables(width)
    plain = np.kron(gz, gy)
    bent = np.kron(gz, sy) + np.kron(sz, gy)
    zy = -(SIGMA * SIGMA) * np.concatenate([plain, bent], axis=0)
    zy = np.concatenate(split(zy), axis=0)
    x = np.concatenate(split(np.concatenate([sx.T, gx.T], axis=0)), axis=1)
    return zy, x


def iota(shape, dim):
    return lax.broadcasted_iota(jnp.int32, shape, dim)


def dot(a, b):
    return jnp.dot(a, b, preferred_element_type=F32)


def kernel(sizes, img, shifts_h, fractions_h, valid_h, counts_h, w1h, w2h, out, shifts, fractions, valid, counts, ext, send, recv, halo_out, halo_in,
           w1, w2, diff, shifted, yhi, ylo, acc, row_a, row_b, recv_a, recv_b, inv,
           load_sem, w_sem, send_sem, recv_sem, halo_ssem, halo_rsem, red_ssem, red_rsem, z_in, y_in):
    rounds, bricks, zs, ys, voxels = sizes
    channels, area, width = ext.shape[1:]
    me = lax.axis_index("round")
    col = lax.axis_index("brick")
    z = lax.rem(col, zs)
    y = col // zs

    last = lax.axis_size("brick")
    right, left = lax.rem(col + 1, last), lax.rem(col + last - 1, last)

    loads = [pltpu.make_async_copy(img.at[k], ext.at[k + 1], load_sem.at[k]) for k in range(bricks)]
    small = ((shifts_h, shifts), (fractions_h, fractions), (valid_h, valid), (w1h, w1), (w2h, w2), (counts_h, counts))
    loads = [pltpu.make_async_copy(a, b, w_sem.at[i]) for i, (a, b) in enumerate(small)] + loads
    for c in loads:
        c.start()

    line = [{"brick": y * zs + lax.rem(z + d, zs)} for d in range(1, zs)]
    plane = [
        {"round": lax.rem(me + a, rounds), "brick": lax.rem(y + b, ys) * zs + z}
        for b in range(ys) for a in range(rounds) if a or b]
    def along_z(d):
        return {"brick": y * zs + lax.rem(z + d + zs, zs)}

    def along_y(d):
        return {"brick": lax.rem(y + d + ys, ys) * zs + z}

    near = [{"round": lax.rem(me + a, rounds)} for a in range(1, rounds)] + [{"brick": right}, {"brick": left}]
    near += [along_z(1), along_z(-1), along_y(1), along_y(-1)]

    def tell(sem, peers):
        for peer in peers:
            pl.semaphore_signal(sem, inc=1, device_id=peer, device_id_type=MESH)

    barrier = pltpu.get_barrier_semaphore()
    tell(barrier, near)

    shape = (width, 2 * width)
    lane = iota(shape, 1)
    diff[...] = iota(shape, 0) - (lane & (width - 1)) + (lane >> 7)
    acc[...] = jnp.zeros_like(acc)
    for c in loads:
        c.wait()

    def pack_mask(shape, packed, long, start):
        p, q = iota(shape, packed), iota(shape, long)
        return jnp.where((p >> 5) * width + start + (p & (HALO - 1)) == q, 1.0, 0.0).astype(BF16)

    def flat(k):
        return jnp.concatenate([ext[k, c] for c in range(channels)], axis=1)

    halo_out[0] = dot(flat(bricks), pack_mask((channels * width, width), 1, 0, width - HALO)).astype(BF16)
    halo_out[1] = dot(flat(1), pack_mask((channels * width, width), 1, 0, 0)).astype(BF16)

    halos = [
        pltpu.make_async_remote_copy(
            src_ref=halo_out.at[i], dst_ref=halo_in.at[i], send_sem=halo_ssem.at[i], recv_sem=halo_rsem.at[i],
            device_id={"brick": j}, device_id_type=MESH)
        for i, j in ((0, right), (1, left))
    ]
    def unpack_halos():
        for i, (slot, start) in enumerate(((0, width - HALO), (bricks + 1, 0))):
            halos[i].wait_recv()
            wide = dot(halo_in[i], pack_mask((width, channels * width), 0, 1, start)).astype(BF16)
            for c in range(channels):
                ext[slot, c] = wide[:, c * width:(c + 1) * width]

    chip, core = me // 2, lax.rem(me, 2)
    chips = rounds // 2

    def brick_of(step):
        turn = lax.rem(step, 3)
        late = step // 3
        ahead = jnp.where(turn == 2, 2, jnp.where(turn == core, 1, chips - 1))
        there = lax.rem(chip + ahead, chips)
        first = jnp.where(there < chips // 2, 1, 0)
        far = 2 * there + jnp.where(late == 0, first, 1 - first)
        return jnp.where(step < 6, far, jnp.where(step == 6, 2 * chip + 1 - core, me))

    groups = ((0, area // 2), (area // 2, area // 4), (3 * area // 4, area // 4))

    def bulk(k, g):
        rows = pl.ds(*groups[g])
        return pltpu.make_async_remote_copy(
            src_ref=send.at[k, :, rows], dst_ref=recv.at[me, :, rows], send_sem=send_sem.at[k, g],
            recv_sem=recv_sem.at[me, g], device_id={"round": k}, device_id_type=MESH)

    def filter_brick(k):
        s = shifts[0, k]
        f = fractions[0, k]
        here = col * bricks + k
        v_left = jnp.where(here > 0, valid[jnp.maximum(here - 1, 0)], 0)
        v_right = jnp.where(here < last * bricks - 1, valid[jnp.minimum(here + 1, last * bricks - 1)], 0)
        v_here = valid[here].astype(F32)
        v_next = jnp.where(s >= 0, v_left, v_right).astype(F32)
        t_next = jnp.where(s >= 0, width, -width) - s
        pick = jnp.concatenate([
            jnp.where(diff[...] == -s, v_here, 0.0).astype(BF16),
            jnp.where(diff[...] == t_next, v_next, 0.0).astype(BF16)], axis=0)
        flat_rows = (channels * area, width)
        is_left = jnp.where(s >= 0, 1.0, 0.0).astype(BF16)
        is_right = jnp.where(s >= 0, 0.0, 1.0).astype(BF16)
        beside = ext[k].reshape(flat_rows) * is_left + ext[k + 2].reshape(flat_rows) * is_right
        moved = dot(jnp.concatenate([ext[k + 1].reshape(flat_rows), beside], axis=1), pick)
        shifted[...] = ((1.0 - f) * moved[:, :width] + f * moved[:, width:]).astype(BF16)
        field = jnp.concatenate([shifted[c * area:(c + 1) * area] for c in range(channels)], axis=1)
        planes = dot(w1[:2 * area], field) + dot(w1[2 * area:], field)
        for c in range(channels):
            both = jnp.concatenate([
                planes[:area, c * width:(c + 1) * width], planes[area:, c * width:(c + 1) * width]], axis=1)
            high = both.astype(BF16)
            yhi[c * area:(c + 1) * area] = high
            ylo[c * area:(c + 1) * area] = (both - high.astype(F32)).astype(BF16)
        twice = dot(yhi[...], w2[...])
        result = (twice[:, :width] + twice[:, width:] + dot(ylo[...], w2[:, :width])).astype(BF16)
        send[k] = result.reshape(channels, area, width)
        size = jnp.abs(result.astype(F32)).reshape(channels, area // 8, 8, width)
        acc[...] += jnp.sum(size, axis=1) * v_here

    def step_body(step, _):
        @pl.when(step == 3)
        def _():
            unpack_halos()

        k = brick_of(step)
        filter_brick(k)

        @pl.when(step == 0)
        def _():
            pl.semaphore_wait(barrier, len(near))
            for c in halos:
                c.start()
            tell(z_in.at[0], [along_z(1), along_z(-1)])
            tell(y_in.at[0], [along_y(1), along_y(-1)])

        @pl.when(step < rounds - 1)
        def _():
            bulk(k, 0).start()

        @pl.when(step == 2)
        def _():
            pl.semaphore_wait(z_in.at[0], 2)
            tell(z_in.at[1], [along_z(2), along_z(-2)])
            pl.semaphore_wait(y_in.at[0], 2)
            tell(y_in.at[1], [along_y(2)])

        @pl.when(step == 4)
        def _():
            pl.semaphore_wait(z_in.at[1], 2)
            tell(z_in.at[2], [along_z(4), along_z(-4)])

        return 0

    lax.fori_loop(0, rounds, step_body, 0)

    def spread(row, slots, slot_of, peers, index):
        for d, peer in enumerate(peers):
            pltpu.make_async_remote_copy(
                src_ref=row, dst_ref=slots.at[pl.ds(slot_of(d), 1)], send_sem=red_ssem.at[index],
                recv_sem=red_rsem.at[index], device_id=peer, device_id_type=MESH).start()

    def arrived(slots, peers, index):
        every = slots.at[pl.ds(0, len(peers))]
        pltpu.make_async_copy(every, every, red_rsem.at[index]).wait()

    sums = jnp.sum(jnp.sum(acc[...], axis=1), axis=1, keepdims=True)
    group = iota((1, width), 1) // (width // channels)
    row_a[...] = sum(jnp.where(group == c, sums[c:c + 1], 0.0) for c in range(channels))
    pl.semaphore_wait(z_in.at[2], 2)
    spread(row_a, recv_a, lambda d: d, line, 0)
    later = [(step, g) for g in (1, 2) for step in [rounds - 2] + list(range(rounds - 2))]
    held = rounds - 1 + 3
    for step, g in later[:held]:
        bulk(brick_of(step), g).start()
    recv[me] = send[me]
    arrived(recv_a, line, 0)
    row_b[...] = row_a[...] + jnp.sum(recv_a[:len(line)], axis=0, keepdims=True)
    pl.semaphore_wait(y_in.at[1], 1)
    spread(row_b, recv_b, lambda d: (d + 1) // rounds * rounds + me, plane, 1)
    for step, g in later[held:]:
        bulk(brick_of(step), g).start()
    arrived(recv_b, plane, 1)
    recv_b[pl.ds(me, 1)] = row_b[...]
    count = jnp.maximum(jnp.sum(counts[...].astype(F32)), 1.0)
    total = jnp.sum(recv_b[...].reshape(ys, rounds, width), axis=0)
    scale = 1.0 / (total / (count * voxels) + 1e-06)
    for c in range(channels):
        lane = c * (width // channels)
        inv[c] = jnp.broadcast_to(scale[:, lane:lane + 1], (rounds, width))

    def norm_body(i, _):
        rows = pl.ds(pl.multiple_of(i * 16, 16), 16)
        energy = jnp.zeros((16, width), F32)
        for r in range(rounds):
            for c in range(channels):
                a = recv[r, c, rows].astype(F32) * inv[c, r:r + 1]
                energy += a * a
        root = lax.rsqrt(energy * (1.0 / (rounds * channels)) + 1.0)
        for r in range(rounds):
            for c in range(channels):
                a = recv[r, c, rows].astype(F32) * inv[c, r:r + 1]
                out[r, c, rows] = (a * root).astype(BF16)
        return 0

    for g, (start, size) in enumerate(groups):
        for d in range(1, rounds):
            source = lax.rem(me + d, rounds)
            piece = recv.at[source, :, pl.ds(start, size)]
            pltpu.make_async_copy(piece, piece, recv_sem.at[source, g]).wait()
        lax.fori_loop(start // 16, (start + size) // 16, norm_body, 0)

    for c in halos:
        c.wait_send()
    for d in range(1, rounds):
        k = lax.rem(me + d, rounds)
        for g in range(len(groups)):
            bulk(k, g).wait_send()
    for index, (slots, peers) in enumerate(((recv_a, line), (recv_b, plane))):
        every = slots.at[pl.ds(0, len(peers))]
        pltpu.make_async_copy(every, every, red_ssem.at[index]).wait()


def on_device(image, shifts, fractions, valid):
    _, bricks, channels, depth, height, width = image.shape
    rounds = lax.axis_size("round")
    zs, ys = 16, 4
    area = depth * height
    w1, w2 = weights(depth, height, width)
    remote = pl.BlockSpec(memory_space=pltpu.HBM)
    vector = pl.BlockSpec(memory_space=pltpu.VMEM)
    tile = (8, width)
    sems = pltpu.SemaphoreType.DMA
    out = pl.pallas_call(
        functools.partial(kernel, (rounds, bricks, zs, ys, depth * height * width)),
        out_shape=jax.ShapeDtypeStruct((rounds, channels, area, width), BF16),
        in_specs=[remote] * 7,
        out_specs=vector,
        scratch_shapes=[
            pltpu.SMEM(shifts.shape, jnp.int32),
            pltpu.SMEM(fractions.shape, F32),
            pltpu.SMEM(valid.shape, jnp.int32),
            pltpu.VMEM((valid.size // width, width), jnp.int32),
            pltpu.VMEM((bricks + 2, channels, area, width), BF16),
            pltpu.VMEM((bricks, channels, area, width), BF16),
            pltpu.VMEM((rounds, channels, area, width), BF16),
            pltpu.VMEM((2, area, width), BF16),
            pltpu.VMEM((2, area, width), BF16),
            pltpu.VMEM(w1.shape, BF16),
            pltpu.VMEM(w2.shape, BF16),
            pltpu.VMEM((width, 2 * width), jnp.int32),
            pltpu.VMEM((channels * area, width), BF16),
            pltpu.VMEM((channels * area, 2 * width), BF16),
            pltpu.VMEM((channels * area, 2 * width), BF16),
            pltpu.VMEM((channels,) + tile, F32),
            pltpu.VMEM((1, width), F32),
            pltpu.VMEM((1, width), F32),
            pltpu.VMEM((zs, width), F32),
            pltpu.VMEM((ys * rounds, width), F32),
            pltpu.VMEM((channels, rounds, width), F32),
            sems((bricks,)), sems((6,)), sems((bricks, 3)), sems((rounds, 3)), sems((2,)), sems((2,)), sems((2,)),
            sems((2,)), pltpu.SemaphoreType.REGULAR((3,)), pltpu.SemaphoreType.REGULAR((2,)),
        ],
        compiler_params=pltpu.CompilerParams(
            collective_id=0, has_side_effects=True, vmem_limit_bytes=48 * 2**20),
        name="spots",
    )(*[pltpu.with_memory_space_constraint(a, pltpu.HBM) for a in (
        image.reshape(bricks, channels, area, width), shifts, fractions, valid, valid.reshape(-1, width),
        jnp.asarray(w1), jnp.asarray(w2))])
    return out.reshape(rounds, 1, 1, channels, depth, height, width)


def solution(mesh):
    return jax.shard_map(
        on_device,
        mesh=mesh,
        in_specs=(P("round", "brick"), P("round", "brick"), P("round", "brick"), P()),
        out_specs=P(None, "round", "brick"),
        check_vma=False,
    )
```

```python
import functools
import math

import jax
import jax.numpy as jnp
import ml_dtypes
import numpy as np
from jax import lax
from jax.experimental import pallas as pl
from jax.experimental.pallas import tpu as pltpu
from jax.sharding import PartitionSpec as P

MESH = pl.DeviceIdType.MESH
SIGMA = 1.5
HALO = 32
BF16 = jnp.bfloat16
F32 = jnp.float32


def tables(count):
    index = np.arange(count, dtype=np.float64)
    offset = index[:, None] - index[None, :]
    smooth = np.exp(-offset * offset / (2.0 * SIGMA * SIGMA)) / (math.sqrt(2.0 * math.pi) * SIGMA)
    smooth = np.where(np.abs(offset) < 4.0 * SIGMA, smooth, 0.0)
    curve = (offset * offset / SIGMA**4 - 1.0 / SIGMA**2) * smooth
    return smooth, curve


def split(matrix):
    high = matrix.astype(ml_dtypes.bfloat16)
    low = (matrix - high.astype(np.float64)).astype(ml_dtypes.bfloat16)
    return high, low


def weights(depth, height, width):
    gz, sz = tables(depth)
    gy, sy = tables(height)
    gx, sx = tables(width)
    plain = np.kron(gz, gy)
    bent = np.kron(gz, sy) + np.kron(sz, gy)
    zy = -(SIGMA * SIGMA) * np.concatenate([plain, bent], axis=0)
    zy = np.concatenate(split(zy), axis=0)
    x = np.concatenate(split(np.concatenate([sx.T, gx.T], axis=0)), axis=1)
    return zy, x


def iota(shape, dim):
    return lax.broadcasted_iota(jnp.int32, shape, dim)


def dot(a, b):
    return jnp.dot(a, b, preferred_element_type=F32)


def kernel(sizes, img, shifts_h, fractions_h, valid_h, counts_h, w1h, w2h, out, shifts, fractions, valid, counts, ext, send, recv, halo_out, halo_in,
           w1, w2, shifted, yhi, ylo, acc, row_a, row_b, recv_a, recv_b, inv,
           load_sem, w_sem, send_sem, recv_sem, halo_ssem, halo_rsem, red_ssem, red_rsem, z_in, y_in):
    rounds, bricks, zs, ys, voxels = sizes
    channels, area, width = ext.shape[1:]
    me = lax.axis_index("round")
    col = lax.axis_index("brick")
    z = lax.rem(col, zs)
    y = col // zs

    last = lax.axis_size("brick")
    right, left = lax.rem(col + 1, last), lax.rem(col + last - 1, last)

    small = ((shifts_h, shifts), (fractions_h, fractions), (valid_h, valid), (w1h, w1), (w2h, w2), (counts_h, counts))
    order = [0, bricks - 1] + list(range(1, bricks - 1))
    loads = [pltpu.make_async_copy(img.at[k], ext.at[k + 1], load_sem.at[k]) for k in order]
    loads += [pltpu.make_async_copy(a, b, w_sem.at[i]) for i, (a, b) in enumerate(small)]
    for c in loads:
        c.start()

    line = [{"brick": y * zs + lax.rem(z + d, zs)} for d in range(1, zs)]
    plane = [
        {"round": lax.rem(me + a, rounds), "brick": lax.rem(y + b, ys) * zs + z}
        for b in range(ys) for a in range(rounds) if a or b]

    def along_z(d):
        return {"brick": y * zs + lax.rem(z + d + zs, zs)}

    def along_y(d):
        return {"brick": lax.rem(y + d + ys, ys) * zs + z}

    near = [{"round": lax.rem(me + a, rounds)} for a in range(1, rounds)] + [{"brick": right}, {"brick": left}]
    near += [along_z(1), along_z(-1), along_y(1), along_y(-1)]

    def tell(sem, peers):
        for peer in peers:
            pl.semaphore_signal(sem, inc=1, device_id=peer, device_id_type=MESH)

    barrier = pltpu.get_barrier_semaphore()
    tell(barrier, near)

    acc[...] = jnp.zeros_like(acc)
    loads[0].wait()
    loads[1].wait()

    def pack_mask(shape, packed, long, start):
        p, q = iota(shape, packed), iota(shape, long)
        return jnp.where((p >> 5) * width + start + (p & (HALO - 1)) == q, 1.0, 0.0).astype(BF16)

    def flat(k):
        return jnp.concatenate([ext[k, c] for c in range(channels)], axis=1)

    halo_out[0] = dot(flat(bricks), pack_mask((channels * width, width), 1, 0, width - HALO)).astype(BF16)
    halo_out[1] = dot(flat(1), pack_mask((channels * width, width), 1, 0, 0)).astype(BF16)

    pl.semaphore_wait(barrier, len(near))
    halos = [
        pltpu.make_async_remote_copy(
            src_ref=halo_out.at[i], dst_ref=halo_in.at[i], send_sem=halo_ssem.at[i], recv_sem=halo_rsem.at[i],
            device_id={"brick": j}, device_id_type=MESH)
        for i, j in ((0, right), (1, left))
    ]
    for c in halos:
        c.start()
    tell(z_in.at[0], [along_z(1), along_z(-1)])
    tell(y_in.at[0], [along_y(1), along_y(-1)])
    for c in loads[2:]:
        c.wait()

    def unpack_halos():
        for i, (slot, start) in enumerate(((0, width - HALO), (bricks + 1, 0))):
            halos[i].wait_recv()
            wide = dot(halo_in[i], pack_mask((width, channels * width), 0, 1, start)).astype(BF16)
            for c in range(channels):
                ext[slot, c] = wide[:, c * width:(c + 1) * width]

    chip, core = me // 2, lax.rem(me, 2)
    chips = rounds // 2

    def brick_of(step):
        turn = lax.rem(step, 3)
        late = step // 3
        ahead = jnp.where(turn == 2, 2, jnp.where(turn == core, 1, chips - 1))
        there = lax.rem(chip + ahead, chips)
        first = jnp.where(there < chips // 2, 1, 0)
        far = 2 * there + jnp.where(late == 0, first, 1 - first)
        return jnp.where(step < 6, far, jnp.where(step == 6, 2 * chip + 1 - core, me))

    groups = ((0, area // 2), (area // 2, area // 4), (3 * area // 4, area // 4))

    def bulk(k, g):
        rows = pl.ds(*groups[g])
        return pltpu.make_async_remote_copy(
            src_ref=send.at[k, :, rows], dst_ref=recv.at[me, :, rows], send_sem=send_sem.at[k, g],
            recv_sem=recv_sem.at[me, g], device_id={"round": k}, device_id_type=MESH)

    def filter_brick(k):
        s = shifts[0, k]
        f = fractions[0, k]
        here = col * bricks + k
        v_left = jnp.where(here > 0, valid[jnp.maximum(here - 1, 0)], 0)
        v_right = jnp.where(here < last * bricks - 1, valid[jnp.minimum(here + 1, last * bricks - 1)], 0)
        v_here = valid[here].astype(F32)
        v_next = jnp.where(s >= 0, v_left, v_right).astype(F32)
        ahead = s >= 0
        turn = jnp.where(ahead, width - s, -s)
        v_low, v_high = jnp.where(ahead, v_here, v_next), jnp.where(ahead, v_next, v_here)
        lane = iota((1, width), 1)
        here_part = (1.0 - f) * jnp.where(lane >= turn, v_high, v_low)
        back_part = f * jnp.where(jnp.where(lane == 0, width, lane) >= turn, v_high, v_low)
        lane = iota((area, width), 1)
        is_left = jnp.where(ahead, 1.0, 0.0).astype(BF16)
        is_right = jnp.where(ahead, 0.0, 1.0).astype(BF16)
        for c in range(channels):
            beside = ext[k, c] * is_left + ext[k + 2, c] * is_right
            low, high = jnp.where(ahead, ext[k + 1, c], beside), jnp.where(ahead, beside, ext[k + 1, c])
            at = jnp.where(lane >= turn, high, low).astype(F32)
            back = pltpu.roll(jnp.where(lane + 1 >= turn, high, low).astype(F32), 1, 1)
            mixed = at * here_part + back * back_part
            shifted[c * area:(c + 1) * area] = pltpu.roll(mixed, lax.rem(s + width, width), 1).astype(BF16)
        for first in range(0, channels, 2):
            field = jnp.concatenate([shifted[c * area:(c + 1) * area] for c in (first, first + 1)], axis=1)
            for part in range(2):
                planes = dot(w1[part * area:(part + 1) * area], field)
                planes += dot(w1[(2 + part) * area:(3 + part) * area], field)
                high = planes.astype(BF16)
                low = (planes - high.astype(F32)).astype(BF16)
                columns = slice(part * width, (part + 1) * width)
                for q in range(2):
                    rows = slice((first + q) * area, (first + q + 1) * area)
                    yhi[rows, columns] = high[:, q * width:(q + 1) * width]
                    ylo[rows, columns] = low[:, q * width:(q + 1) * width]
        for c in range(channels):
            rows = slice(c * area, (c + 1) * area)
            twice = dot(yhi[rows], w2[...])
            result = (twice[:, :width] + twice[:, width:] + dot(ylo[rows], w2[:, :width])).astype(BF16)
            send[k, c] = result
            size = jnp.abs(result.astype(F32)).reshape(area // 8, 8, width)
            acc[c] += jnp.sum(size, axis=0) * v_here

    def step_body(step, _):
        @pl.when(step == 3)
        def _():
            unpack_halos()

        k = brick_of(step)
        filter_brick(k)

        @pl.when(step < rounds - 1)
        def _():
            bulk(k, 0).start()

        @pl.when(step == 2)
        def _():
            pl.semaphore_wait(z_in.at[0], 2)
            tell(z_in.at[1], [along_z(2), along_z(-2)])
            pl.semaphore_wait(y_in.at[0], 2)
            tell(y_in.at[1], [along_y(2)])

        @pl.when(step == 4)
        def _():
            pl.semaphore_wait(z_in.at[1], 2)
            tell(z_in.at[2], [along_z(4), along_z(-4)])

        return 0

    lax.fori_loop(0, rounds, step_body, 0)

    def spread(row, slots, slot_of, peers, index):
        for d, peer in enumerate(peers):
            pltpu.make_async_remote_copy(
                src_ref=row, dst_ref=slots.at[pl.ds(slot_of(d), 1)], send_sem=red_ssem.at[index],
                recv_sem=red_rsem.at[index], device_id=peer, device_id_type=MESH).start()

    def arrived(slots, peers, index):
        every = slots.at[pl.ds(0, len(peers))]
        pltpu.make_async_copy(every, every, red_rsem.at[index]).wait()

    sums = jnp.sum(jnp.sum(acc[...], axis=1), axis=1, keepdims=True)
    group = iota((1, width), 1) // (width // channels)
    row_a[...] = sum(jnp.where(group == c, sums[c:c + 1], 0.0) for c in range(channels))
    pl.semaphore_wait(z_in.at[2], 2)
    spread(row_a, recv_a, lambda d: d, line, 0)
    later = [(step, g) for g in (1, 2) for step in [rounds - 2] + list(range(rounds - 2))]
    held = 5
    for step, g in later[:held]:
        bulk(brick_of(step), g).start()
    recv[me] = send[me]
    arrived(recv_a, line, 0)
    row_b[...] = row_a[...] + jnp.sum(recv_a[:len(line)], axis=0, keepdims=True)
    pl.semaphore_wait(y_in.at[1], 1)
    spread(row_b, recv_b, lambda d: (d + 1) // rounds * rounds + me, plane, 1)
    for step, g in later[held:]:
        bulk(brick_of(step), g).start()
    arrived(recv_b, plane, 1)
    recv_b[pl.ds(me, 1)] = row_b[...]
    count = jnp.maximum(jnp.sum(counts[...].astype(F32)), 1.0)
    total = jnp.sum(recv_b[...].reshape(ys, rounds, width), axis=0)
    scale = 1.0 / (total / (count * voxels) + 1e-06)
    for c in range(channels):
        lane = c * (width // channels)
        inv[c] = jnp.broadcast_to(scale[:, lane:lane + 1], (rounds, width))

    def norm_body(i, _):
        rows = pl.ds(pl.multiple_of(i * 16, 16), 16)
        energy = jnp.zeros((16, width), F32)
        for r in range(rounds):
            for c in range(channels):
                a = recv[r, c, rows].astype(F32) * inv[c, r:r + 1]
                energy += a * a
        root = lax.rsqrt(energy * (1.0 / (rounds * channels)) + 1.0)
        for r in range(rounds):
            for c in range(channels):
                a = recv[r, c, rows].astype(F32) * inv[c, r:r + 1]
                out[r, c, rows] = (a * root).astype(BF16)
        return 0

    for g, (start, size) in enumerate(groups):
        for d in range(1, rounds):
            source = lax.rem(me + d, rounds)
            piece = recv.at[source, :, pl.ds(start, size)]
            pltpu.make_async_copy(piece, piece, recv_sem.at[source, g]).wait()
        lax.fori_loop(start // 16, (start + size) // 16, norm_body, 0)

    for c in halos:
        c.wait_send()
    for d in range(1, rounds):
        k = lax.rem(me + d, rounds)
        for g in range(len(groups)):
            bulk(k, g).wait_send()
    for index, (slots, peers) in enumerate(((recv_a, line), (recv_b, plane))):
        every = slots.at[pl.ds(0, len(peers))]
        pltpu.make_async_copy(every, every, red_ssem.at[index]).wait()


def on_device(image, shifts, fractions, valid):
    _, bricks, channels, depth, height, width = image.shape
    rounds = lax.axis_size("round")
    zs, ys = 16, 4
    area = depth * height
    w1, w2 = weights(depth, height, width)
    remote = pl.BlockSpec(memory_space=pltpu.HBM)
    vector = pl.BlockSpec(memory_space=pltpu.VMEM)
    tile = (8, width)
    sems = pltpu.SemaphoreType.DMA
    out = pl.pallas_call(
        functools.partial(kernel, (rounds, bricks, zs, ys, depth * height * width)),
        out_shape=jax.ShapeDtypeStruct((rounds, channels, area, width), BF16),
        in_specs=[remote] * 7,
        out_specs=vector,
        scratch_shapes=[
            pltpu.SMEM(shifts.shape, jnp.int32),
            pltpu.SMEM(fractions.shape, F32),
            pltpu.SMEM(valid.shape, jnp.int32),
            pltpu.VMEM((valid.size // width, width), jnp.int32),
            pltpu.VMEM((bricks + 2, channels, area, width), BF16),
            pltpu.VMEM((bricks, channels, area, width), BF16),
            pltpu.VMEM((rounds, channels, area, width), BF16),
            pltpu.VMEM((2, area, width), BF16),
            pltpu.VMEM((2, area, width), BF16),
            pltpu.VMEM(w1.shape, BF16),
            pltpu.VMEM(w2.shape, BF16),
            pltpu.VMEM((channels * area, width), BF16),
            pltpu.VMEM((channels * area, 2 * width), BF16),
            pltpu.VMEM((channels * area, 2 * width), BF16),
            pltpu.VMEM((channels,) + tile, F32),
            pltpu.VMEM((1, width), F32),
            pltpu.VMEM((1, width), F32),
            pltpu.VMEM((zs, width), F32),
            pltpu.VMEM((ys * rounds, width), F32),
            pltpu.VMEM((channels, rounds, width), F32),
            sems((bricks,)), sems((6,)), sems((bricks, 3)), sems((rounds, 3)), sems((2,)), sems((2,)), sems((2,)),
            sems((2,)), pltpu.SemaphoreType.REGULAR((3,)), pltpu.SemaphoreType.REGULAR((2,)),
        ],
        compiler_params=pltpu.CompilerParams(
            collective_id=0, has_side_effects=True, vmem_limit_bytes=48 * 2**20),
        name="spots",
    )(*[pltpu.with_memory_space_constraint(a, pltpu.HBM) for a in (
        image.reshape(bricks, channels, area, width), shifts, fractions, valid, valid.reshape(-1, width),
        jnp.asarray(w1), jnp.asarray(w2))])
    return out.reshape(rounds, 1, 1, channels, depth, height, width)


def solution(mesh):
    return jax.shard_map(
        on_device,
        mesh=mesh,
        in_specs=(P("round", "brick"), P("round", "brick"), P("round", "brick"), P()),
        out_specs=P(None, "round", "brick"),
        check_vma=False,
    )
```

```python
import functools
import math

import jax
import jax.numpy as jnp
import ml_dtypes
import numpy as np
from jax import lax
from jax.experimental import pallas as pl
from jax.experimental.pallas import tpu as pltpu
from jax.sharding import PartitionSpec as P

MESH = pl.DeviceIdType.MESH
SIGMA = 1.5
HALO = 32
BF16 = jnp.bfloat16
F32 = jnp.float32


def tables(count):
    index = np.arange(count, dtype=np.float64)
    offset = index[:, None] - index[None, :]
    smooth = np.exp(-offset * offset / (2.0 * SIGMA * SIGMA)) / (math.sqrt(2.0 * math.pi) * SIGMA)
    smooth = np.where(np.abs(offset) < 4.0 * SIGMA, smooth, 0.0)
    curve = (offset * offset / SIGMA**4 - 1.0 / SIGMA**2) * smooth
    return smooth, curve


def split(matrix):
    high = matrix.astype(ml_dtypes.bfloat16)
    low = (matrix - high.astype(np.float64)).astype(ml_dtypes.bfloat16)
    return high, low


def weights(depth, height, width):
    gz, sz = tables(depth)
    gy, sy = tables(height)
    gx, sx = tables(width)
    plain = np.kron(gz, gy)
    bent = np.kron(gz, sy) + np.kron(sz, gy)
    zy = -(SIGMA * SIGMA) * np.concatenate([plain, bent], axis=0)
    zy = np.concatenate(split(zy), axis=0)
    x = np.concatenate(split(np.concatenate([sx.T, gx.T], axis=0)), axis=1)
    return zy, x


def iota(shape, dim):
    return lax.broadcasted_iota(jnp.int32, shape, dim)


def dot(a, b):
    return jnp.dot(a, b, preferred_element_type=F32)


def kernel(sizes, img, shifts_h, fractions_h, valid_h, counts_h, w1h, w2h, out, shifts, fractions, valid, counts, ext, send, recv, halo_out, halo_in,
           w1, w2, masks, shifted, yhi, ylo, acc, row_a, row_b, recv_a, recv_b, inv,
           load_sem, w_sem, send_sem, recv_sem, halo_ssem, halo_rsem, red_ssem, red_rsem, z_in, y_in):
    rounds, bricks, zs, ys, voxels = sizes
    channels, area, width = ext.shape[1:]
    me = lax.axis_index("round")
    col = lax.axis_index("brick")
    z = lax.rem(col, zs)
    y = col // zs

    last = lax.axis_size("brick")
    right, left = lax.rem(col + 1, last), lax.rem(col + last - 1, last)

    small = ((shifts_h, shifts), (fractions_h, fractions), (valid_h, valid), (w1h, w1), (w2h, w2), (counts_h, counts))
    order = [0, bricks - 1] + list(range(1, bricks - 1))
    loads = [pltpu.make_async_copy(img.at[k], ext.at[k + 1], load_sem.at[k]) for k in order]
    loads += [pltpu.make_async_copy(a, b, w_sem.at[i]) for i, (a, b) in enumerate(small)]
    for c in loads:
        c.start()

    line = [{"brick": y * zs + lax.rem(z + d, zs)} for d in range(1, zs)]
    plane = [
        {"round": lax.rem(me + a, rounds), "brick": lax.rem(y + b, ys) * zs + z}
        for b in range(ys) for a in range(rounds) if a or b]

    def along_z(d):
        return {"brick": y * zs + lax.rem(z + d + zs, zs)}

    def along_y(d):
        return {"brick": lax.rem(y + d + ys, ys) * zs + z}

    near = [{"round": lax.rem(me + a, rounds)} for a in range(1, rounds)] + [{"brick": right}, {"brick": left}]
    near += [along_z(1), along_z(-1), along_y(1), along_y(-1)]

    def tell(sem, peers):
        for peer in peers:
            pl.semaphore_signal(sem, inc=1, device_id=peer, device_id_type=MESH)

    barrier = pltpu.get_barrier_semaphore()
    tell(barrier, near)

    acc[...] = jnp.zeros_like(acc)
    long, packed = iota(masks.shape[1:], 0), iota(masks.shape[1:], 1)
    for i, start in enumerate((width - HALO, 0)):
        place = (packed >> 5) * width + start + (packed & (HALO - 1))
        masks[i] = jnp.where(place == long, 1.0, 0.0).astype(BF16)
    for c in loads:
        c.wait()

    halos = [
        pltpu.make_async_remote_copy(
            src_ref=halo_out.at[i], dst_ref=halo_in.at[i], send_sem=halo_ssem.at[i], recv_sem=halo_rsem.at[i],
            device_id={"brick": j}, device_id_type=MESH)
        for i, j in ((0, right), (1, left))
    ]

    def send_halos():
        for i, slot in enumerate((bricks, 1)):
            strip = jnp.concatenate([ext[slot, c] for c in range(channels)], axis=1)
            halo_out[i] = dot(strip, masks[i]).astype(BF16)
            halos[i].start()

    def unpack_halos():
        for i, slot in enumerate((0, bricks + 1)):
            halos[i].wait_recv()
            wide = lax.dot_general(
                halo_in[i], masks[i], (((1,), (1,)), ((), ())), preferred_element_type=F32).astype(BF16)
            for c in range(channels):
                ext[slot, c] = wide[:, c * width:(c + 1) * width]

    chip, core = me // 2, lax.rem(me, 2)
    chips = rounds // 2

    def brick_of(step):
        turn = lax.rem(step, 3)
        late = step // 3
        ahead = jnp.where(turn == 2, 2, jnp.where(turn == core, 1, chips - 1))
        there = lax.rem(chip + ahead, chips)
        first = jnp.where(there < chips // 2, 1, 0)
        far = 2 * there + jnp.where(late == 0, first, 1 - first)
        return jnp.where(step < 6, far, jnp.where(step == 6, 2 * chip + 1 - core, me))

    groups = ((0, area // 2), (area // 2, area // 4), (3 * area // 4, area // 4))

    def bulk(k, g):
        rows = pl.ds(*groups[g])
        return pltpu.make_async_remote_copy(
            src_ref=send.at[k, :, rows], dst_ref=recv.at[me, :, rows], send_sem=send_sem.at[k, g],
            recv_sem=recv_sem.at[me, g], device_id={"round": k}, device_id_type=MESH)

    def filter_brick(k):
        s = shifts[0, k]
        f = fractions[0, k]
        here = col * bricks + k
        v_left = jnp.where(here > 0, valid[jnp.maximum(here - 1, 0)], 0)
        v_right = jnp.where(here < last * bricks - 1, valid[jnp.minimum(here + 1, last * bricks - 1)], 0)
        v_here = valid[here].astype(F32)
        v_next = jnp.where(s >= 0, v_left, v_right).astype(F32)
        ahead = s >= 0
        turn = jnp.where(ahead, width - s, -s)
        v_low, v_high = jnp.where(ahead, v_here, v_next), jnp.where(ahead, v_next, v_here)
        lane = iota((1, width), 1)
        here_part = (1.0 - f) * jnp.where(lane >= turn, v_high, v_low)
        back_part = f * jnp.where(jnp.where(lane == 0, width, lane) >= turn, v_high, v_low)
        lane = iota((area, width), 1)
        is_left = jnp.where(ahead, 1.0, 0.0).astype(BF16)
        is_right = jnp.where(ahead, 0.0, 1.0).astype(BF16)
        for c in range(channels):
            beside = ext[k, c] * is_left + ext[k + 2, c] * is_right
            low, high = jnp.where(ahead, ext[k + 1, c], beside), jnp.where(ahead, beside, ext[k + 1, c])
            at = jnp.where(lane >= turn, high, low).astype(F32)
            back = pltpu.roll(jnp.where(lane + 1 >= turn, high, low).astype(F32), 1, 1)
            mixed = at * here_part + back * back_part
            shifted[c * area:(c + 1) * area] = pltpu.roll(mixed, lax.rem(s + width, width), 1).astype(BF16)
        for first in range(0, channels, 2):
            field = jnp.concatenate([shifted[c * area:(c + 1) * area] for c in (first, first + 1)], axis=1)
            for part in range(2):
                planes = dot(w1[part * area:(part + 1) * area], field)
                planes += dot(w1[(2 + part) * area:(3 + part) * area], field)
                high = planes.astype(BF16)
                low = (planes - high.astype(F32)).astype(BF16)
                columns = slice(part * width, (part + 1) * width)
                for q in range(2):
                    rows = slice((first + q) * area, (first + q + 1) * area)
                    yhi[rows, columns] = high[:, q * width:(q + 1) * width]
                    ylo[rows, columns] = low[:, q * width:(q + 1) * width]
        for c in range(channels):
            rows = slice(c * area, (c + 1) * area)
            twice = dot(yhi[rows], w2[...])
            result = (twice[:, :width] + twice[:, width:] + dot(ylo[rows], w2[:, :width])).astype(BF16)
            send[k, c] = result
            size = jnp.abs(result.astype(F32)).reshape(area // 8, 8, width)
            acc[c] += jnp.sum(size, axis=0) * v_here

    def step_body(step, _):
        @pl.when(step == 3)
        def _():
            unpack_halos()

        k = brick_of(step)
        filter_brick(k)

        @pl.when(step == 0)
        def _():
            pl.semaphore_wait(barrier, len(near))

        @pl.when(step < rounds - 1)
        def _():
            bulk(k, 0).start()

        @pl.when(step == 0)
        def _():
            send_halos()
            tell(z_in.at[0], [along_z(1), along_z(-1)])
            tell(y_in.at[0], [along_y(1), along_y(-1)])

        @pl.when(step == 2)
        def _():
            pl.semaphore_wait(z_in.at[0], 2)
            tell(z_in.at[1], [along_z(2), along_z(-2)])
            pl.semaphore_wait(y_in.at[0], 2)
            tell(y_in.at[1], [along_y(2)])

        @pl.when(step == 4)
        def _():
            pl.semaphore_wait(z_in.at[1], 2)
            tell(z_in.at[2], [along_z(4), along_z(-4)])

        return 0

    lax.fori_loop(0, rounds, step_body, 0)

    def spread(row, slots, slot_of, peers, index):
        for d, peer in enumerate(peers):
            pltpu.make_async_remote_copy(
                src_ref=row, dst_ref=slots.at[pl.ds(slot_of(d), 1)], send_sem=red_ssem.at[index],
                recv_sem=red_rsem.at[index], device_id=peer, device_id_type=MESH).start()

    def arrived(slots, peers, index):
        every = slots.at[pl.ds(0, len(peers))]
        pltpu.make_async_copy(every, every, red_rsem.at[index]).wait()

    sums = jnp.sum(jnp.sum(acc[...], axis=1), axis=1, keepdims=True)
    group = iota((1, width), 1) // (width // channels)
    row_a[...] = sum(jnp.where(group == c, sums[c:c + 1], 0.0) for c in range(channels))
    pl.semaphore_wait(z_in.at[2], 2)
    spread(row_a, recv_a, lambda d: d, line, 0)
    later = [(step, g) for g in (1, 2) for step in [rounds - 2] + list(range(rounds - 2))]
    held = 5
    for step, g in later[:held]:
        bulk(brick_of(step), g).start()
    recv[me] = send[me]
    arrived(recv_a, line, 0)
    row_b[...] = row_a[...] + jnp.sum(recv_a[:len(line)], axis=0, keepdims=True)
    pl.semaphore_wait(y_in.at[1], 1)
    spread(row_b, recv_b, lambda d: (d + 1) // rounds * rounds + me, plane, 1)
    for step, g in later[held:]:
        bulk(brick_of(step), g).start()
    arrived(recv_b, plane, 1)
    recv_b[pl.ds(me, 1)] = row_b[...]
    count = jnp.maximum(jnp.sum(counts[...].astype(F32)), 1.0)
    total = jnp.sum(recv_b[...].reshape(ys, rounds, width), axis=0)
    scale = 1.0 / (total / (count * voxels) + 1e-06)
    for c in range(channels):
        lane = c * (width // channels)
        inv[c] = jnp.broadcast_to(scale[:, lane:lane + 1], (rounds, width))

    def norm_body(i, _):
        rows = pl.ds(pl.multiple_of(i * 16, 16), 16)
        energy = jnp.zeros((16, width), F32)
        for r in range(rounds):
            for c in range(channels):
                a = recv[r, c, rows].astype(F32) * inv[c, r:r + 1]
                energy += a * a
        root = lax.rsqrt(energy * (1.0 / (rounds * channels)) + 1.0)
        for r in range(rounds):
            for c in range(channels):
                a = recv[r, c, rows].astype(F32) * inv[c, r:r + 1]
                out[r, c, rows] = (a * root).astype(BF16)
        return 0

    for g, (start, size) in enumerate(groups):
        for d in range(1, rounds):
            source = lax.rem(me + d, rounds)
            piece = recv.at[source, :, pl.ds(start, size)]
            pltpu.make_async_copy(piece, piece, recv_sem.at[source, g]).wait()
        lax.fori_loop(start // 16, (start + size) // 16, norm_body, 0)

    for c in halos:
        c.wait_send()
    for d in range(1, rounds):
        k = lax.rem(me + d, rounds)
        for g in range(len(groups)):
            bulk(k, g).wait_send()
    for index, (slots, peers) in enumerate(((recv_a, line), (recv_b, plane))):
        every = slots.at[pl.ds(0, len(peers))]
        pltpu.make_async_copy(every, every, red_ssem.at[index]).wait()


def on_device(image, shifts, fractions, valid):
    _, bricks, channels, depth, height, width = image.shape
    rounds = lax.axis_size("round")
    zs, ys = 16, 4
    area = depth * height
    w1, w2 = weights(depth, height, width)
    remote = pl.BlockSpec(memory_space=pltpu.HBM)
    vector = pl.BlockSpec(memory_space=pltpu.VMEM)
    tile = (8, width)
    sems = pltpu.SemaphoreType.DMA
    out = pl.pallas_call(
        functools.partial(kernel, (rounds, bricks, zs, ys, depth * height * width)),
        out_shape=jax.ShapeDtypeStruct((rounds, channels, area, width), BF16),
        in_specs=[remote] * 7,
        out_specs=vector,
        scratch_shapes=[
            pltpu.SMEM(shifts.shape, jnp.int32),
            pltpu.SMEM(fractions.shape, F32),
            pltpu.SMEM(valid.shape, jnp.int32),
            pltpu.VMEM((valid.size // width, width), jnp.int32),
            pltpu.VMEM((bricks + 2, channels, area, width), BF16),
            pltpu.VMEM((bricks, channels, area, width), BF16),
            pltpu.VMEM((rounds, channels, area, width), BF16),
            pltpu.VMEM((2, area, width), BF16),
            pltpu.VMEM((2, area, width), BF16),
            pltpu.VMEM(w1.shape, BF16),
            pltpu.VMEM(w2.shape, BF16),
            pltpu.VMEM((2, channels * width, width), BF16),
            pltpu.VMEM((channels * area, width), BF16),
            pltpu.VMEM((channels * area, 2 * width), BF16),
            pltpu.VMEM((channels * area, 2 * width), BF16),
            pltpu.VMEM((channels,) + tile, F32),
            pltpu.VMEM((1, width), F32),
            pltpu.VMEM((1, width), F32),
            pltpu.VMEM((zs, width), F32),
            pltpu.VMEM((ys * rounds, width), F32),
            pltpu.VMEM((channels, rounds, width), F32),
            sems((bricks,)), sems((6,)), sems((bricks, 3)), sems((rounds, 3)), sems((2,)), sems((2,)), sems((2,)),
            sems((2,)), pltpu.SemaphoreType.REGULAR((3,)), pltpu.SemaphoreType.REGULAR((2,)),
        ],
        compiler_params=pltpu.CompilerParams(
            collective_id=0, has_side_effects=True, vmem_limit_bytes=48 * 2**20),
        name="spots",
    )(*[pltpu.with_memory_space_constraint(a, pltpu.HBM) for a in (
        image.reshape(bricks, channels, area, width), shifts, fractions, valid, valid.reshape(-1, width),
        jnp.asarray(w1), jnp.asarray(w2))])
    return out.reshape(rounds, 1, 1, channels, depth, height, width)


def solution(mesh):
    return jax.shard_map(
        on_device,
        mesh=mesh,
        in_specs=(P("round", "brick"), P("round", "brick"), P("round", "brick"), P()),
        out_specs=P(None, "round", "brick"),
        check_vma=False,
    )
```

```python
import functools
import math

import jax
import jax.numpy as jnp
import ml_dtypes
import numpy as np
from jax import lax
from jax.experimental import pallas as pl
from jax.experimental.pallas import tpu as pltpu
from jax.sharding import PartitionSpec as P

MESH = pl.DeviceIdType.MESH
SIGMA = 1.5
HALO = 32
BF16 = jnp.bfloat16
F32 = jnp.float32


def tables(count):
    index = np.arange(count, dtype=np.float64)
    offset = index[:, None] - index[None, :]
    smooth = np.exp(-offset * offset / (2.0 * SIGMA * SIGMA)) / (math.sqrt(2.0 * math.pi) * SIGMA)
    smooth = np.where(np.abs(offset) < 4.0 * SIGMA, smooth, 0.0)
    curve = (offset * offset / SIGMA**4 - 1.0 / SIGMA**2) * smooth
    return smooth, curve


def split(matrix):
    high = matrix.astype(ml_dtypes.bfloat16)
    low = (matrix - high.astype(np.float64)).astype(ml_dtypes.bfloat16)
    return high, low


def weights(depth, height, width):
    gz, sz = tables(depth)
    gy, sy = tables(height)
    gx, sx = tables(width)
    plain = np.kron(gz, gy)
    bent = np.kron(gz, sy) + np.kron(sz, gy)
    zy = -(SIGMA * SIGMA) * np.concatenate([plain, bent], axis=0)
    zy = np.concatenate(split(zy), axis=0)
    x = np.concatenate(split(np.concatenate([sx.T, gx.T], axis=0)), axis=1)
    return zy, x


def iota(shape, dim):
    return lax.broadcasted_iota(jnp.int32, shape, dim)


def dot(a, b):
    return jnp.dot(a, b, preferred_element_type=F32)


def kernel(sizes, img, shifts_h, fractions_h, valid_h, counts_h, w1h, w2h, out, shifts, fractions, valid, counts, ext, send, recv, halo_out, halo_in,
           w1, w2, masks, shifted, yhi, ylo, acc, row_a, row_b, recv_a, recv_b, inv,
           load_sem, w_sem, send_sem, recv_sem, halo_ssem, halo_rsem, red_ssem, red_rsem, z_in, y_in):
    rounds, bricks, zs, ys, voxels = sizes
    channels, area, width = ext.shape[1:]
    me = lax.axis_index("round")
    col = lax.axis_index("brick")
    z = lax.rem(col, zs)
    y = col // zs

    last = lax.axis_size("brick")
    right, left = lax.rem(col + 1, last), lax.rem(col + last - 1, last)

    small = ((shifts_h, shifts), (fractions_h, fractions), (valid_h, valid), (w1h, w1), (w2h, w2), (counts_h, counts))
    order = [0, bricks - 1] + list(range(1, bricks - 1))
    loads = [pltpu.make_async_copy(img.at[k], ext.at[k + 1], load_sem.at[k]) for k in order]
    loads += [pltpu.make_async_copy(a, b, w_sem.at[i]) for i, (a, b) in enumerate(small)]
    line = [{"brick": y * zs + lax.rem(z + d, zs)} for d in range(1, zs)]
    plane = [
        {"round": lax.rem(me + a, rounds), "brick": lax.rem(y + b, ys) * zs + z}
        for b in range(ys) for a in range(rounds) if a or b]

    def along_z(d):
        return {"brick": y * zs + lax.rem(z + d + zs, zs)}

    def along_y(d):
        return {"brick": lax.rem(y + d + ys, ys) * zs + z}

    near = [{"round": lax.rem(me + a, rounds)} for a in range(1, rounds)] + [{"brick": right}, {"brick": left}]
    near += [along_z(1), along_z(-1), along_y(1), along_y(-1)]

    def tell(sem, peers):
        for peer in peers:
            pl.semaphore_signal(sem, inc=1, device_id=peer, device_id_type=MESH)

    barrier = pltpu.get_barrier_semaphore()
    tell(barrier, near)

    for c in loads:
        c.start()

    acc[...] = jnp.zeros_like(acc)
    long, packed = iota(masks.shape[1:], 0), iota(masks.shape[1:], 1)
    for i, start in enumerate((width - HALO, 0)):
        place = (packed >> 5) * width + start + (packed & (HALO - 1))
        masks[i] = jnp.where(place == long, 1.0, 0.0).astype(BF16)
    for c in loads:
        c.wait()

    halos = [
        pltpu.make_async_remote_copy(
            src_ref=halo_out.at[i], dst_ref=halo_in.at[i], send_sem=halo_ssem.at[i], recv_sem=halo_rsem.at[i],
            device_id={"brick": j}, device_id_type=MESH)
        for i, j in ((0, right), (1, left))
    ]

    def send_halos():
        for i, slot in enumerate((bricks, 1)):
            strip = jnp.concatenate([ext[slot, c] for c in range(channels)], axis=1)
            halo_out[i] = dot(strip, masks[i]).astype(BF16)
            halos[i].start()

    def unpack_halos():
        for i, slot in enumerate((0, bricks + 1)):
            halos[i].wait_recv()
            wide = lax.dot_general(
                halo_in[i], masks[i], (((1,), (1,)), ((), ())), preferred_element_type=F32).astype(BF16)
            for c in range(channels):
                ext[slot, c] = wide[:, c * width:(c + 1) * width]

    chip, core = me // 2, lax.rem(me, 2)
    chips = rounds // 2

    def brick_of(step):
        turn = lax.rem(step, 3)
        late = step // 3
        ahead = jnp.where(turn == 2, 2, jnp.where(turn == core, 1, chips - 1))
        there = lax.rem(chip + ahead, chips)
        first = jnp.where(there < chips // 2, 1, 0)
        far = 2 * there + jnp.where(late == 0, first, 1 - first)
        return jnp.where(step < 6, far, jnp.where(step == 6, 2 * chip + 1 - core, me))

    groups = ((0, area // 2), (area // 2, area // 4), (3 * area // 4, area // 4))

    def bulk(k, g):
        rows = pl.ds(*groups[g])
        return pltpu.make_async_remote_copy(
            src_ref=send.at[k, :, rows], dst_ref=recv.at[me, :, rows], send_sem=send_sem.at[k, g],
            recv_sem=recv_sem.at[me, g], device_id={"round": k}, device_id_type=MESH)

    def filter_brick(k):
        s = shifts[0, k]
        f = fractions[0, k]
        here = col * bricks + k
        v_left = jnp.where(here > 0, valid[jnp.maximum(here - 1, 0)], 0)
        v_right = jnp.where(here < last * bricks - 1, valid[jnp.minimum(here + 1, last * bricks - 1)], 0)
        v_here = valid[here].astype(F32)
        v_next = jnp.where(s >= 0, v_left, v_right).astype(F32)
        ahead = s >= 0
        turn = jnp.where(ahead, width - s, -s)
        v_low, v_high = jnp.where(ahead, v_here, v_next), jnp.where(ahead, v_next, v_here)
        lane = iota((1, width), 1)
        here_part = (1.0 - f) * jnp.where(lane >= turn, v_high, v_low)
        back_part = f * jnp.where(jnp.where(lane == 0, width, lane) >= turn, v_high, v_low)
        lane = iota((area, width), 1)
        is_left = jnp.where(ahead, 1.0, 0.0).astype(BF16)
        is_right = jnp.where(ahead, 0.0, 1.0).astype(BF16)
        for c in range(channels):
            beside = ext[k, c] * is_left + ext[k + 2, c] * is_right
            low, high = jnp.where(ahead, ext[k + 1, c], beside), jnp.where(ahead, beside, ext[k + 1, c])
            at = jnp.where(lane >= turn, high, low).astype(F32)
            back = pltpu.roll(jnp.where(lane + 1 >= turn, high, low).astype(F32), 1, 1)
            mixed = at * here_part + back * back_part
            shifted[c * area:(c + 1) * area] = pltpu.roll(mixed, lax.rem(s + width, width), 1).astype(BF16)
        for first in range(0, channels, 2):
            field = jnp.concatenate([shifted[c * area:(c + 1) * area] for c in (first, first + 1)], axis=1)
            for part in range(2):
                planes = dot(w1[part * area:(part + 1) * area], field)
                planes += dot(w1[(2 + part) * area:(3 + part) * area], field)
                high = planes.astype(BF16)
                low = (planes - high.astype(F32)).astype(BF16)
                columns = slice(part * width, (part + 1) * width)
                for q in range(2):
                    rows = slice((first + q) * area, (first + q + 1) * area)
                    yhi[rows, columns] = high[:, q * width:(q + 1) * width]
                    ylo[rows, columns] = low[:, q * width:(q + 1) * width]
        for c in range(channels):
            rows = slice(c * area, (c + 1) * area)
            twice = dot(yhi[rows], w2[...])
            result = (twice[:, :width] + twice[:, width:] + dot(ylo[rows], w2[:, :width])).astype(BF16)
            send[k, c] = result
            size = jnp.abs(result.astype(F32)).reshape(area // 8, 8, width)
            acc[c] += jnp.sum(size, axis=0) * v_here

    def step_body(step, _):
        @pl.when(step == 3)
        def _():
            unpack_halos()

        k = brick_of(step)
        filter_brick(k)

        @pl.when(step == 0)
        def _():
            pl.semaphore_wait(barrier, len(near))

        @pl.when(step < rounds - 1)
        def _():
            bulk(k, 0).start()

        @pl.when(step == 0)
        def _():
            send_halos()
            tell(z_in.at[0], [along_z(1), along_z(-1)])
            tell(y_in.at[0], [along_y(1), along_y(-1)])

        @pl.when(step == 2)
        def _():
            pl.semaphore_wait(z_in.at[0], 2)
            tell(z_in.at[1], [along_z(2), along_z(-2)])
            pl.semaphore_wait(y_in.at[0], 2)
            tell(y_in.at[1], [along_y(2)])

        @pl.when(step == 4)
        def _():
            pl.semaphore_wait(z_in.at[1], 2)
            tell(z_in.at[2], [along_z(4), along_z(-4)])

        return 0

    lax.fori_loop(0, rounds, step_body, 0)

    def spread(row, slots, slot_of, peers, index):
        for d, peer in enumerate(peers):
            pltpu.make_async_remote_copy(
                src_ref=row, dst_ref=slots.at[pl.ds(slot_of(d), 1)], send_sem=red_ssem.at[index],
                recv_sem=red_rsem.at[index], device_id=peer, device_id_type=MESH).start()

    def arrived(slots, peers, index):
        every = slots.at[pl.ds(0, len(peers))]
        pltpu.make_async_copy(every, every, red_rsem.at[index]).wait()

    sums = jnp.sum(jnp.sum(acc[...], axis=1), axis=1, keepdims=True)
    group = iota((1, width), 1) // (width // channels)
    row_a[...] = sum(jnp.where(group == c, sums[c:c + 1], 0.0) for c in range(channels))
    pl.semaphore_wait(z_in.at[2], 2)
    spread(row_a, recv_a, lambda d: d, line, 0)
    later = [(step, g) for g in (1, 2) for step in [rounds - 2] + list(range(rounds - 2))]
    held = 5
    for step, g in later[:held]:
        bulk(brick_of(step), g).start()
    recv[me] = send[me]
    arrived(recv_a, line, 0)
    row_b[...] = row_a[...] + jnp.sum(recv_a[:len(line)], axis=0, keepdims=True)
    pl.semaphore_wait(y_in.at[1], 1)
    spread(row_b, recv_b, lambda d: (d + 1) // rounds * rounds + me, plane, 1)
    for step, g in later[held:]:
        bulk(brick_of(step), g).start()
    arrived(recv_b, plane, 1)
    recv_b[pl.ds(me, 1)] = row_b[...]
    count = jnp.maximum(jnp.sum(counts[...].astype(F32)), 1.0)
    total = jnp.sum(recv_b[...].reshape(ys, rounds, width), axis=0)
    scale = 1.0 / (total / (count * voxels) + 1e-06)
    for c in range(channels):
        lane = c * (width // channels)
        inv[c] = jnp.broadcast_to(scale[:, lane:lane + 1], (rounds, width))

    def norm_body(i, _):
        rows = pl.ds(pl.multiple_of(i * 16, 16), 16)
        energy = jnp.zeros((16, width), F32)
        for r in range(rounds):
            for c in range(channels):
                a = recv[r, c, rows].astype(F32) * inv[c, r:r + 1]
                energy += a * a
        root = lax.rsqrt(energy * (1.0 / (rounds * channels)) + 1.0)
        for r in range(rounds):
            for c in range(channels):
                a = recv[r, c, rows].astype(F32) * inv[c, r:r + 1]
                out[r, c, rows] = (a * root).astype(BF16)
        return 0

    for g, (start, size) in enumerate(groups):
        for d in range(1, rounds):
            source = lax.rem(me + d, rounds)
            piece = recv.at[source, :, pl.ds(start, size)]
            pltpu.make_async_copy(piece, piece, recv_sem.at[source, g]).wait()
        lax.fori_loop(start // 16, (start + size) // 16, norm_body, 0)

    for c in halos:
        c.wait_send()
    for d in range(1, rounds):
        k = lax.rem(me + d, rounds)
        for g in range(len(groups)):
            bulk(k, g).wait_send()
    for index, (slots, peers) in enumerate(((recv_a, line), (recv_b, plane))):
        every = slots.at[pl.ds(0, len(peers))]
        pltpu.make_async_copy(every, every, red_ssem.at[index]).wait()


def on_device(image, shifts, fractions, valid):
    _, bricks, channels, depth, height, width = image.shape
    rounds = lax.axis_size("round")
    zs, ys = 16, 4
    area = depth * height
    w1, w2 = weights(depth, height, width)
    remote = pl.BlockSpec(memory_space=pltpu.HBM)
    vector = pl.BlockSpec(memory_space=pltpu.VMEM)
    tile = (8, width)
    sems = pltpu.SemaphoreType.DMA
    out = pl.pallas_call(
        functools.partial(kernel, (rounds, bricks, zs, ys, depth * height * width)),
        out_shape=jax.ShapeDtypeStruct((rounds, channels, area, width), BF16),
        in_specs=[remote] * 7,
        out_specs=vector,
        scratch_shapes=[
            pltpu.SMEM(shifts.shape, jnp.int32),
            pltpu.SMEM(fractions.shape, F32),
            pltpu.SMEM(valid.shape, jnp.int32),
            pltpu.VMEM((valid.size // width, width), jnp.int32),
            pltpu.VMEM((bricks + 2, channels, area, width), BF16),
            pltpu.VMEM((bricks, channels, area, width), BF16),
            pltpu.VMEM((rounds, channels, area, width), BF16),
            pltpu.VMEM((2, area, width), BF16),
            pltpu.VMEM((2, area, width), BF16),
            pltpu.VMEM(w1.shape, BF16),
            pltpu.VMEM(w2.shape, BF16),
            pltpu.VMEM((2, channels * width, width), BF16),
            pltpu.VMEM((channels * area, width), BF16),
            pltpu.VMEM((channels * area, 2 * width), BF16),
            pltpu.VMEM((channels * area, 2 * width), BF16),
            pltpu.VMEM((channels,) + tile, F32),
            pltpu.VMEM((1, width), F32),
            pltpu.VMEM((1, width), F32),
            pltpu.VMEM((zs, width), F32),
            pltpu.VMEM((ys * rounds, width), F32),
            pltpu.VMEM((channels, rounds, width), F32),
            sems((bricks,)), sems((6,)), sems((bricks, 3)), sems((rounds, 3)), sems((2,)), sems((2,)), sems((2,)),
            sems((2,)), pltpu.SemaphoreType.REGULAR((3,)), pltpu.SemaphoreType.REGULAR((2,)),
        ],
        compiler_params=pltpu.CompilerParams(
            collective_id=0, has_side_effects=True, vmem_limit_bytes=48 * 2**20),
        name="spots",
    )(*[pltpu.with_memory_space_constraint(a, pltpu.HBM) for a in (
        image.reshape(bricks, channels, area, width), shifts, fractions, valid, valid.reshape(-1, width),
        jnp.asarray(w1), jnp.asarray(w2))])
    return out.reshape(rounds, 1, 1, channels, depth, height, width)


def solution(mesh):
    return jax.shard_map(
        on_device,
        mesh=mesh,
        in_specs=(P("round", "brick"), P("round", "brick"), P("round", "brick"), P()),
        out_specs=P(None, "round", "brick"),
        check_vma=False,
    )
```
